32 devices in a mesh: groups: 2 (over x), redist: 4 (over y, core), contract: 4 (over z).
Axes of the slice: x: 2, y: 2, z: 4, core: 2. Of those that a mesh axis runs over, the one named last changes fastest.
Arguments:
- amplitudes: float32 [2048, 24576], P(('groups', 'redist'), 'contract'), parts along dimension 0, may hold values from -6 to 6
- pair_irrep: int32 [2048, 1], P(('groups', 'redist')), parts along dimension 0, may hold values from 0 to 7; in each aligned block of 256 rows (0 to 255, 256 to 511, ...) at most 64 rows name the same one
- integrals: float32 [24576, 8192], P('contract', 'redist'), may hold values from -0.0390625 to 0.0390625
Outputs:
- ladder: float32 [2048, 1024], P(('groups', 'redist')), parts along dimension 0
The draws below stay inside these ranges and needn't reach their ends.
There are 2 independent parts, one for each index of `groups`. The reference program is written for one: setup_inputs(seed, part) draws one part's arguments, and reference() takes and returns one part's arrays. A program takes and returns all parts, laid end to end along the dimension named above; an argument that names none is the same for every part. Nothing has to cross between parts.
Inputs may be any that keep to these rules, and one draw needn't show every extreme that they name: `pair_irrep`: among the pairs of one device (aligned blocks of 256 rows) no irrep occurs more than 64 times, and some irrep occurs exactly 64 times.
All inputs are finite; a program needn't handle non-finite values.
Results may differ from the reference program's by a relative error of at most 0.0001.
Values sent between devices are 32-bit elements; how exact they have to be, the bound alone decides.
No kernel may reach another device: no remote copies, remote signals or barrier semaphores. Data moves between devices by JAX's collectives and lax.ppermute only.
A program may use at most 256 MiB of HBM per device.

```python
import math
import jax
import jax.numpy as jnp
import numpy as np
from jax import lax

PAIR_DEV = 256
KB = 24576
ABB = 1024
CAP = 64
PAIRS = 1024


def block_scale(own_key, dims, cuts, low, largest):
    factor_of = 1.0
    for axis_at, parts in cuts:
        draws = jax.random.uniform(jax.random.fold_in(jax.random.fold_in(own_key, 6), axis_at), (parts,), jnp.float32, low / len(cuts), largest / len(cuts))
        factor_of = factor_of * jnp.repeat(jnp.exp(draws), dims[axis_at] // parts).reshape((-1,) + (1,) * (len(dims) - 1 - axis_at))
    return factor_of


def deal_out(own_key, own, number, rows, number_of, top, limit, skew):
    ranking = jax.random.permutation(own_key, number_of)
    packed, usual = load_shares(number_of, rows * top, limit, skew, True), load_shares(number_of, rows * top, limit, skew, False)
    places = jnp.arange(number_of)

    def named(lengths, rotation):
        used = int((lengths > 0).sum())
        fixed = max(1, used // 4)
        passed = fixed + (places - fixed + rotation * (used - fixed)) % max(1, number_of - fixed)
        return jnp.zeros((number_of,), jnp.int32).at[ranking[jnp.where(places < fixed, places, passed)]].set(jnp.asarray(lengths, jnp.int32))

    lengths = jnp.where(number % 4 == 0, named(packed, number // 4), named(usual, number - number // 4 - 1))
    mixed = jax.random.permutation(jax.random.fold_in(own, 3), number_of)
    source_of, receiver = mixed[0:number_of // 2 * 2:2], mixed[1:number_of // 2 * 2:2]
    slack = jnp.minimum(lengths[source_of] - 1, limit - lengths[receiver]) // 2
    slack = jnp.where((source_of == ranking[0]) | (receiver == ranking[0]) | (lengths[receiver] == 0), 0, jnp.maximum(slack, 0))
    passed = jax.random.randint(jax.random.fold_in(own, 4), (number_of // 2,), 0, 1 << 20) % (slack + 1)
    lengths = lengths.at[source_of].add(-passed).at[receiver].add(passed)
    items = jnp.searchsorted(jnp.cumsum(lengths), jnp.arange(rows * top), side="right").astype(jnp.int32)
    grid = items.reshape(top, rows).T
    grid = grid[jax.random.permutation(jax.random.fold_in(own, 1), rows)]
    rotation = jax.random.randint(jax.random.fold_in(own, 2), (rows, 1), 0, top)
    return jnp.take_along_axis(grid, (jnp.arange(top)[None, :] + rotation) % top, axis=1)


def load_shares(count, total, reach, slope, full):
    loads = [(1 << 20) // math.isqrt(rank ** slope) + 1 for rank in range(1, count + 1)]
    largest = reach if full else min(reach, max(-(-total // count), total * loads[0] // sum(loads)))
    least = 1 if total - largest >= count - 1 else 0
    holding, surplus = [largest] + [least] * (count - 1), total - largest - least * (count - 1)
    while surplus > 0:
        free = [i for i in range(1, count) if holding[i] < largest] or [i for i in range(1, count) if holding[i] < reach]
        whole, budget = sum([loads[i] for i in free]), surplus
        for i in free:
            more = min(reach - holding[i], max(1, budget * loads[i] // whole), surplus)
            holding[i] = holding[i] + more
            surplus = surplus - more
    return np.array(holding)


def centred(key, dims, deviation, limit, split=(), dtype=jnp.bfloat16):
    values = jax.random.normal(key, dims, jnp.float32) * deviation
    if len(split) > 0:
        values = block_scale(key, dims, split, -0.22, 0.18) * values
    return jnp.clip(values, min=-limit, max=limit).astype(dtype)


def setup_inputs(seed: int = 0, part: int = 0) -> dict:
    key_list = jax.random.split(jax.random.key(seed), 4)
    part_splits = jax.random.split(jax.random.fold_in(key_list[3], part), 4)
    amplitudes = centred(part_splits[0], (PAIRS, KB), 1.0, 6.0, ((0, 4), (1, 4)), jnp.float32)
    pair_irrep_keys = jax.random.split(jax.random.fold_in(part_splits[1], 1), PAIRS // PAIR_DEV)
    pair_irrep_turns = jax.random.permutation(jax.random.fold_in(part_splits[1], 3), PAIRS // PAIR_DEV)
    pair_irrep = jax.vmap(lambda own, number: deal_out(jax.random.fold_in(part_splits[1], 2), own, number, PAIR_DEV, 8, 1, CAP, 2))(pair_irrep_keys, pair_irrep_turns).reshape((PAIRS, 1))
    integrals = centred(key_list[2], (KB, 8 * ABB), KB ** -0.5, 0.0390625, ((0, 4), (1, 4)), jnp.float32)
    return dict(amplitudes=amplitudes, pair_irrep=pair_irrep, integrals=integrals)


def reference(amplitudes, pair_irrep, integrals):
    labels = pair_irrep[:, 0]
    result = jnp.zeros((amplitudes.shape[0], ABB), jnp.float32)
    for irrep_index in range(8):
        block = integrals[:, irrep_index * ABB:(irrep_index + 1) * ABB]
        product = jnp.dot(amplitudes, block, precision=lax.Precision.HIGHEST, preferred_element_type=jnp.float32)
        result = jnp.where((labels == irrep_index)[:, None], product, result)
    return result
```

```python
import functools

import jax
import jax.numpy as jnp
from jax import lax
from jax.experimental import pallas as pl
from jax.experimental.pallas import tpu as pltpu
from jax.sharding import PartitionSpec as P

IRREPS = 8
F32 = jnp.float32
BF16 = jnp.bfloat16
VMEM_LIMIT = 56 << 20

FIRST = 48
LAST = 48
CLASSES = (112, 128, 144, 160, 176, 192, 256)

dot = functools.partial(jnp.dot, preferred_element_type=F32)


def halves(value):
    high = value.astype(BF16)
    return high, (value - high.astype(F32)).astype(BF16)


def thirds(value):
    high = value.astype(BF16)
    rest = value - high.astype(F32)
    middle = rest.astype(BF16)
    return high, middle, (rest - middle.astype(F32)).astype(BF16)


def product(left, right):
    rows = left.shape[0]
    left_high, left_low = halves(left)
    right_high, right_low = halves(right)
    both = dot(jnp.concatenate([left_high, left_low], 0), right_high)
    return both[:rows] + both[rows:] + dot(left_high, right_low)


def pick(chosen, value):
    high, middle, low = thirds(value)
    return dot(chosen, high) + dot(chosen, middle) + dot(chosen, low)


def params():
    return pltpu.CompilerParams(vmem_limit_bytes=VMEM_LIMIT)


def whole():
    return pl.BlockSpec(memory_space=pltpu.VMEM)


def scalar():
    return pl.BlockSpec(memory_space=pltpu.SMEM)


def ranks_of(labels, place, cap):
    rows = labels.shape[0]

    def kernel(place_ref, labels_ref, row_ref, col_ref, message_ref):
        base = (4 * place_ref[0]).astype(F32)
        core = place_ref[1].astype(F32)
        down = lax.broadcasted_iota(jnp.int32, (rows, rows), 0)
        across = lax.broadcasted_iota(jnp.int32, (rows, rows), 1)
        label_c = labels_ref[...].astype(F32)
        label_r = jnp.sum(jnp.where(down == across, label_c, 0.0), axis=0, keepdims=True)

        def facts(label):
            local = label - base
            stays = (local >= 0) & (local < 4)
            owner = jnp.where(local >= 2, 1.0, 0.0)
            order = jnp.where(owner == core, 0.0, 2.0) + (local - 2 * owner)
            return stays, order * cap

        stays_c, slot_c = facts(label_c)
        stays_r, slot_r = facts(label_r)
        cross_c = jnp.where(stays_c, 0.0, 1.0)
        cross_r = jnp.where(stays_r, 0.0, 1.0)
        alike = jnp.where(label_c == label_r, 1.0, 0.0)
        ahead = down < across
        rank_r = jnp.sum(jnp.where(ahead, cross_c, 0.0), axis=0, keepdims=True)
        rank_c = jnp.sum(jnp.where(across < down, cross_r, 0.0), axis=1, keepdims=True)
        inner_r = jnp.sum(jnp.where(ahead, alike, 0.0), axis=0, keepdims=True)
        inner_c = jnp.sum(jnp.where(across < down, alike, 0.0), axis=1, keepdims=True)
        rank_r = jnp.where(stays_r, -1.0, rank_r)
        rank_c = jnp.where(stays_c, -1.0, rank_c)
        slot_r = jnp.where(stays_r, slot_r + inner_r, -1.0)
        slot_c = jnp.where(stays_c, slot_c + inner_c, -1.0)
        sub = lax.broadcasted_iota(jnp.int32, (8, rows), 0)
        row_ref[...] = jnp.where(sub == 0, rank_r, slot_r)
        lane = lax.broadcasted_iota(jnp.int32, (rows, 128), 1)
        col_ref[...] = jnp.where(lane == 0, rank_c, slot_c)
        sent = jnp.sum(jnp.where(rank_c == across.astype(F32), label_c + 1.0, 0.0), axis=0, keepdims=True) - 1.0
        count = jnp.sum(cross_r, axis=1, keepdims=True)
        message_ref[...] = jnp.where(sub == 0, sent, count)

    return pl.pallas_call(
        kernel,
        in_specs=[scalar(), whole()],
        out_specs=[whole()] * 3,
        out_shape=[
            jax.ShapeDtypeStruct((8, rows), F32),
            jax.ShapeDtypeStruct((rows, 128), F32),
            jax.ShapeDtypeStruct((8, rows), F32),
        ],
        compiler_params=params(),
        name="ranks",
    )(place, labels)


def step_of(width, start=0):
    for step in (1024, 768, 512, 384, 256, 128):
        if width % step == 0 and start % step == 0:
            return step
    return width


def pack(amplitudes, ranks, kind, pieces, start, width):
    rows = amplitudes.shape[0]
    step = step_of(width, start)

    def kernel(ranks_ref, value_ref, *outs):
        high, low = halves(value_ref[...])
        for (offset, count), out in zip(pieces, outs):
            wanted = lax.broadcasted_iota(jnp.int32, (count, rows), 0).astype(F32) + float(offset)
            chosen = jnp.where(ranks_ref[kind : kind + 1, :] == wanted, 1.0, 0.0).astype(BF16)
            out[...] = dot(chosen, high) + dot(chosen, low)

    return pl.pallas_call(
        kernel,
        grid=(width // step,),
        in_specs=[
            pl.BlockSpec((8, rows), lambda k: (0, 0)),
            pl.BlockSpec((rows, step), lambda k: (0, k + start // step)),
        ],
        out_specs=[pl.BlockSpec((count, step), lambda k: (0, k)) for _, count in pieces],
        out_shape=[jax.ShapeDtypeStruct((count, width), F32) for _, count in pieces],
        compiler_params=params(),
        cost_estimate=pl.CostEstimate(flops=4 * rows * width * sum(c for _, c in pieces), bytes_accessed=8 * rows * width, transcendentals=0),
        name="pack",
    )(ranks, amplitudes)


def own_rows(own, mate, integrals):
    slots, width = own.shape
    cap = slots // 2
    cols = integrals.shape[1] // 2
    step = step_of(width)

    def kernel(own_ref, mate_ref, right_ref, own_out, mate_out):
        @pl.when(pl.program_id(0) == 0)
        def _():
            own_out[...] = jnp.zeros_like(own_out)
            mate_out[...] = jnp.zeros_like(mate_out)

        for j in range(2):
            at = slice(j * cap, (j + 1) * cap)
            left = jnp.concatenate([own_ref[at], mate_ref[at]], 0)
            both = product(left, right_ref[:, j * cols : (j + 1) * cols])
            own_out[at] += both[:cap]
            mate_out[at] += both[cap:]

    rows_spec = pl.BlockSpec((slots, step), lambda k: (0, k))
    out_spec = pl.BlockSpec((slots, cols), lambda k: (0, 0))
    out = jax.ShapeDtypeStruct((slots, cols), F32)
    return pl.pallas_call(
        kernel,
        grid=(width // step,),
        in_specs=[rows_spec, rows_spec, pl.BlockSpec((step, 2 * cols), lambda k: (k, 0))],
        out_specs=[out_spec, out_spec],
        out_shape=[out, out],
        compiler_params=params(),
        cost_estimate=pl.CostEstimate(flops=24 * slots * width * cols, bytes_accessed=8 * width * cols, transcendentals=0),
        name="own_rows",
    )(own, mate, integrals)


def crossed_rows(place, labels_own, labels_mate, offset, own, mate, integrals, start, width, totals):
    count = sum(a.shape[0] for a, _ in own)
    cols = integrals.shape[1] // 2
    ranks = labels_own.shape[1]
    step = step_of(width, start)
    for _, first in own:
        step = min(step, step_of(width, first)) if first else step
    parts = len(own)

    def kernel(place_ref, labels_own_ref, labels_mate_ref, *refs):
        own_refs, mate_refs = refs[:parts], refs[parts : 2 * parts]
        right_ref = refs[2 * parts]
        earlier, (own_out, mate_out) = refs[2 * parts + 1 : -2], refs[-2:]

        @pl.when(pl.program_id(0) == 0)
        def _():
            if earlier:
                own_out[...] = earlier[0][...]
                mate_out[...] = earlier[1][...]
            else:
                own_out[...] = jnp.zeros_like(own_out)
                mate_out[...] = jnp.zeros_like(mate_out)

        wanted = lax.broadcasted_iota(jnp.int32, (count, ranks), 0) + offset
        at = lax.broadcasted_iota(jnp.int32, (count, ranks), 1)
        label = jnp.concatenate(
            [jnp.sum(jnp.where(wanted == at, r[0:1, :], 0.0), axis=1, keepdims=True) for r in (labels_own_ref, labels_mate_ref)], 0
        )
        value = jnp.concatenate([r[...] for r in own_refs + mate_refs], 0)
        first_irrep = (4 * place_ref[0] + 2 * place_ref[1]).astype(F32)
        both = jnp.zeros((2 * count, cols), F32)
        for j in range(2):
            left = jnp.where(label == first_irrep + float(j), value, 0.0)
            both = both + product(left, right_ref[:, j * cols : (j + 1) * cols])
        own_out[...] += both[:count]
        mate_out[...] += both[count:]

    def piece(array, first):
        return pl.BlockSpec((array.shape[0], step), lambda k: (0, k + first // step))

    label_spec = pl.BlockSpec((8, ranks), lambda k: (0, 0))
    out_spec = pl.BlockSpec((count, cols), lambda k: (0, 0))
    out = jax.ShapeDtypeStruct((count, cols), F32)
    earlier = [] if totals is None else list(totals)
    at_total = 4 + 2 * parts
    return pl.pallas_call(
        kernel,
        grid=(width // step,),
        in_specs=[scalar(), label_spec, label_spec]
        + [piece(a, f) for a, f in own + mate]
        + [pl.BlockSpec((step, 2 * cols), lambda k: (k + start // step, 0))]
        + [out_spec] * len(earlier),
        out_specs=[out_spec, out_spec],
        out_shape=[out, out],
        input_output_aliases={at_total + i: i for i in range(len(earlier))},
        compiler_params=params(),
        cost_estimate=pl.CostEstimate(flops=24 * count * width * cols, bytes_accessed=8 * width * cols, transcendentals=0),
        name="crossed_rows",
    )(place, labels_own, labels_mate, *[a for a, _ in own + mate], integrals, *earlier)


def spread(place, own, other, devices):
    rows, cols = own.shape
    block = cols // devices

    def kernel(place_ref, own_ref, other_ref, *outs):
        for m, out in enumerate(outs):
            at = pl.ds(pl.multiple_of((place_ref[2] ^ m) * block, block), block)
            out[...] = own_ref[:, at] + other_ref[:, at]

    return pl.pallas_call(
        kernel,
        in_specs=[scalar(), whole(), whole()],
        out_specs=[whole()] * devices,
        out_shape=[jax.ShapeDtypeStruct((rows, block), F32)] * devices,
        compiler_params=params(),
        name="spread",
    )(place, own, other)


def assemble(place, columns, kept, blocks):
    rows = columns.shape[0]
    slots, cols = kept.shape
    devices = len(blocks[0][1])
    width = cols // devices

    def kernel(place_ref, columns_ref, kept_ref, *refs):
        out = refs[-1]
        rank, slot = columns_ref[:, 0:1], columns_ref[:, 1:2]

        def chooser(column, offset, count):
            wanted = lax.broadcasted_iota(jnp.int32, (rows, count), 1).astype(F32) + float(offset)
            return jnp.where(column == wanted, 1.0, 0.0).astype(BF16)

        own_rows_chosen = chooser(slot, 0, slots)
        chosen = [chooser(rank, offset, arrays[0].shape[0]) for offset, arrays in blocks]
        for m in range(devices):
            at = pl.ds(pl.multiple_of((place_ref[2] ^ m) * width, width), width)
            total = pick(own_rows_chosen, kept_ref[:, at])
            for b in range(len(blocks)):
                total = total + pick(chosen[b], refs[b * devices + m][...])
            out[:, at] = total

    return pl.pallas_call(
        kernel,
        in_specs=[scalar(), whole(), whole()] + [whole()] * (devices * len(blocks)),
        out_specs=whole(),
        out_shape=jax.ShapeDtypeStruct((rows, cols), F32),
        compiler_params=params(),
        name="assemble",
    )(place, columns, kept, *[a for _, arrays in blocks for a in arrays])


def swap_y(value):
    return lax.ppermute(value, "redist", [(r, r ^ 2) for r in range(4)])


def swap_core(value):
    return lax.ppermute(value, "redist", [(r, r ^ 1) for r in range(4)])


def swap_z(value, m, devices):
    return lax.ppermute(value, "contract", [(z, z ^ m) for z in range(devices)])


def home(value, m, devices):
    pairs = [(r * devices + z, (r ^ 2) * devices + (z ^ m)) for r in range(4) for z in range(devices)]
    return lax.ppermute(value, ("redist", "contract"), pairs)


def reduce_z(place, own, mate, devices):
    blocks = spread(place, own, swap_core(mate), devices)
    total = blocks[0]
    for m in range(1, devices):
        total = total + swap_z(blocks[m], m, devices)
    return total


def rest(total, amplitudes, integrals, place, ranks, columns, labels_own, labels_mate, first_own, first_mate, kept, devices):
    width = amplitudes.shape[1]
    last = min(LAST, (total - FIRST) // 2 // 8 * 8)
    middle = total - FIRST - last
    half = width // 2
    middle_chunks = [(0, half), (half, half)]
    last_chunks = [(0, half), (half, width // 3), (half + width // 3, width - half - width // 3)]
    middle_rows = [swap_y(pack(amplitudes, ranks, 0, [(FIRST, middle)], s, w)[0]) for s, w in middle_chunks]
    last_rows = [swap_y(pack(amplitudes, ranks, 0, [(FIRST + middle, last)], s, w)[0]) for s, w in last_chunks]
    kept = lax.psum(kept, "contract")

    totals = None
    for (start, wide), rows in zip(middle_chunks, middle_rows):
        own = [(first_own, start), (rows, 0)]
        mate = [(first_mate, start), (swap_core(rows), 0)]
        totals = crossed_rows(place, labels_own, labels_mate, 0, own, mate, integrals, start, wide, totals)
    quarter = swap_y(reduce_z(place, *totals, devices))
    middle_back = [quarter] + [swap_z(quarter, m, devices) for m in range(1, devices)]

    totals = None
    for (start, wide), rows in zip(last_chunks, last_rows):
        totals = crossed_rows(
            place, labels_own, labels_mate, FIRST + middle, [(rows, 0)], [(swap_core(rows), 0)], integrals, start, wide, totals
        )
    quarter = reduce_z(place, *totals, devices)
    last_back = [home(quarter, m, devices) for m in range(devices)]
    return assemble(place, columns, kept, [(0, middle_back), (FIRST + middle, last_back)])


def paired(amplitudes, pair_irrep, integrals):
    devices = lax.axis_size("contract")
    rows, width = amplitudes.shape
    cap = rows // 4
    position = lax.axis_index("redist")
    place = jnp.stack([position // 2, position % 2, lax.axis_index("contract")]).astype(jnp.int32)
    ranks, columns, message = ranks_of(pair_irrep, place, cap)

    (first,) = pack(amplitudes, ranks, 0, [(0, FIRST)], 0, width)
    first_own = swap_y(first)
    labels_own = swap_y(message)
    sub = lax.broadcasted_iota(jnp.int32, message.shape, 0)
    labels_own = jnp.where(sub == 1, jnp.maximum(message, labels_own), labels_own)
    labels_mate = swap_core(labels_own)
    most = jnp.maximum(labels_own, labels_mate)[1:2, 0:128]
    groups = lax.axis_size("groups")
    for shift in range(1, groups):
        most = jnp.maximum(most, lax.ppermute(most, "groups", [(g, (g + shift) % groups) for g in range(groups)]))
    classes = [c for c in CLASSES if c < rows] + [rows]
    at = jnp.sum(jnp.asarray(classes, F32) < most[0, 0]).astype(jnp.int32)

    slots_own, slots_mate = pack(amplitudes, ranks, 1, [(0, 2 * cap), (2 * cap, 2 * cap)], 0, width)
    own, mate = own_rows(slots_own, swap_core(slots_mate), integrals)
    kept = jnp.concatenate([own, swap_core(mate)], 0)
    first_mate = swap_core(first_own)

    branches = [functools.partial(rest, c, devices=devices) for c in classes]
    return lax.switch(
        at, branches, amplitudes, integrals, place, ranks, columns, labels_own, labels_mate, first_own, first_mate, kept
    )


def general(amplitudes, pair_irrep, integrals):
    redist_count = lax.axis_size("redist")
    irreps_here = max(1, IRREPS // redist_count)
    copies = max(1, redist_count // IRREPS)
    pair_rows, contract_width = amplitudes.shape
    capacity = pair_rows // 4
    block_cols = integrals.shape[1] // irreps_here
    labels = pair_irrep[:, 0]
    onehot = (labels[:, None] == jnp.arange(IRREPS, dtype=jnp.int32)[None, :]).astype(jnp.int32)
    rank_in = jnp.sum(jnp.cumsum(onehot, axis=0) * onehot, axis=1) - 1
    slot_of = labels * capacity + rank_in
    source_rows = (
        jnp.full((IRREPS * capacity,), pair_rows, jnp.int32).at[slot_of].set(jnp.arange(pair_rows, dtype=jnp.int32))
    )
    source_rows = jnp.repeat(source_rows.reshape(IRREPS, 1, capacity), copies, axis=1).reshape(-1)
    gathered = jnp.take(amplitudes, source_rows, axis=0, mode="fill", fill_value=0.0)
    outgoing = gathered.reshape(redist_count, irreps_here, capacity, contract_width)
    local_cols = integrals.reshape(contract_width, irreps_here, block_cols)
    partial_value = jnp.einsum(
        "risk,kiw->risw",
        lax.all_to_all(outgoing, "redist", split_axis=0, concat_axis=0, tiled=True),
        local_cols,
        precision=lax.Precision.HIGHEST,
        preferred_element_type=F32,
    )
    summed = lax.psum(partial_value, "contract")
    returned = lax.all_to_all(summed, "redist", split_axis=0, concat_axis=0, tiled=True)
    by_irrep = returned.reshape(IRREPS, copies, capacity, block_cols)
    return by_irrep[labels, :, rank_in].reshape(pair_rows, copies * block_cols)


def shards(amplitudes, pair_irrep, integrals):
    rows, width = amplitudes.shape
    devices = lax.axis_size("contract")
    cols = integrals.shape[1] // 2
    fits = lax.axis_size("redist") == 4 and devices in (2, 4) and rows % 64 == 0 and rows > FIRST + LAST + 16
    if fits and width % 3072 == 0 and cols % (128 * devices) == 0:
        return paired(amplitudes, pair_irrep, integrals)
    return general(amplitudes, pair_irrep, integrals)


def solution(mesh):
    return jax.shard_map(
        shards,
        mesh=mesh,
        in_specs=(
            P(("groups", "redist"), "contract"),
            P(("groups", "redist"), None),
            P("contract", "redist"),
        ),
        out_specs=P(("groups", "redist"), None),
        check_vma=False,
    )
```

```python
import functools

import jax
import jax.numpy as jnp
from jax import lax
from jax.experimental import pallas as pl
from jax.experimental.pallas import tpu as pltpu
from jax.sharding import PartitionSpec as P

IRREPS = 8
F32 = jnp.float32
BF16 = jnp.bfloat16

BLOCK = 96
CLASSES = (48, 64, 80, 104)
EIGHTHS = 8
BLOCK_PARTS = (5, 3)
SPARE_PARTS = (3, 3, 2)

BRIEF = pl.CostEstimate(flops=1, bytes_accessed=1, transcendentals=0)

dot = functools.partial(jnp.dot, preferred_element_type=F32)


def halves(value):
    high = value.astype(BF16)
    return high, (value - high.astype(F32)).astype(BF16)


def thirds(value):
    high = value.astype(BF16)
    rest = value - high.astype(F32)
    middle = rest.astype(BF16)
    return high, middle, (rest - middle.astype(F32)).astype(BF16)


def product(left, right):
    rows = left.shape[0]
    left_high, left_low = halves(left)
    right_high, right_low = halves(right)
    both = dot(jnp.concatenate([left_high, left_low], 0), right_high)
    return both[:rows] + both[rows:] + dot(left_high, right_low)


def pick(chosen, value):
    high, middle, low = thirds(value)
    return dot(chosen, high) + dot(chosen, middle) + dot(chosen, low)


def starts_of(parts):
    return [sum(parts[:i]) for i in range(len(parts))]


def params(mebibytes):
    return pltpu.CompilerParams(vmem_limit_bytes=mebibytes << 20)


def whole():
    return pl.BlockSpec(memory_space=pltpu.VMEM)


def scalar():
    return pl.BlockSpec(memory_space=pltpu.SMEM)


def ranks_of(labels, place, cap):
    rows = labels.shape[0]

    def kernel(place_ref, labels_ref, row_ref, col_ref, message_ref):
        base = (4 * place_ref[0]).astype(F32)
        core = place_ref[1].astype(F32)
        down = lax.broadcasted_iota(jnp.int32, (rows, rows), 0)
        across = lax.broadcasted_iota(jnp.int32, (rows, rows), 1)
        label_c = labels_ref[...].astype(F32)
        label_r = jnp.sum(jnp.where(down == across, label_c, 0.0), axis=0, keepdims=True)

        def facts(label):
            local = label - base
            stays = (local >= 0) & (local < 4)
            owner = jnp.where(local >= 2, 1.0, 0.0)
            order = jnp.where(owner == core, 0.0, 2.0) + (local - 2 * owner)
            return stays, order * cap

        stays_c, slot_c = facts(label_c)
        stays_r, slot_r = facts(label_r)
        cross_c = jnp.where(stays_c, 0.0, 1.0)
        cross_r = jnp.where(stays_r, 0.0, 1.0)
        alike = jnp.where(label_c == label_r, 1.0, 0.0)
        ahead = down < across
        rank_r = jnp.sum(jnp.where(ahead, cross_c, 0.0), axis=0, keepdims=True)
        rank_c = jnp.sum(jnp.where(across < down, cross_r, 0.0), axis=1, keepdims=True)
        inner_r = jnp.sum(jnp.where(ahead, alike, 0.0), axis=0, keepdims=True)
        inner_c = jnp.sum(jnp.where(across < down, alike, 0.0), axis=1, keepdims=True)
        rank_r = jnp.where(stays_r, -1.0, rank_r)
        rank_c = jnp.where(stays_c, -1.0, rank_c)
        slot_r = jnp.where(stays_r, slot_r + inner_r, -1.0)
        slot_c = jnp.where(stays_c, slot_c + inner_c, -1.0)
        sub = lax.broadcasted_iota(jnp.int32, (8, rows), 0)
        row_ref[...] = jnp.where(sub == 0, rank_r, slot_r)
        lane = lax.broadcasted_iota(jnp.int32, (rows, 128), 1)
        col_ref[...] = jnp.where(lane == 0, rank_c, slot_c)
        sent = jnp.sum(jnp.where(rank_c == across.astype(F32), label_c + 1.0, 0.0), axis=0, keepdims=True) - 1.0
        count = jnp.sum(cross_r, axis=1, keepdims=True)
        message_ref[...] = jnp.where(sub == 0, sent, count)

    return pl.pallas_call(
        kernel,
        in_specs=[scalar(), whole()],
        out_specs=[whole()] * 3,
        out_shape=[
            jax.ShapeDtypeStruct((8, rows), F32),
            jax.ShapeDtypeStruct((rows, 128), F32),
            jax.ShapeDtypeStruct((8, rows), F32),
        ],
        compiler_params=params(16),
        name="ranks",
    )(place, labels)


def pack(amplitudes, ranks, message, pieces, room, name):
    rows, width = amplitudes.shape
    step = width // EIGHTHS
    first = min(p[3] for p in pieces)
    steps = max(p[3] + p[4] for p in pieces) - first
    extra = [] if message is None else [message]

    def kernel(ranks_ref, value_ref, *refs):
        outs = refs[len(extra) :]
        k = pl.program_id(0) + first
        high, low = halves(value_ref[...])
        for i, ((kind, offset, count, start, parts), out) in enumerate(zip(pieces, outs)):

            @pl.when((k >= start) & (k < start + parts))
            def _():
                wanted = lax.broadcasted_iota(jnp.int32, (count, rows), 0).astype(F32) + float(offset)
                chosen = jnp.where(ranks_ref[kind : kind + 1, :] == wanted, 1.0, 0.0).astype(BF16)
                out[0:count] = dot(chosen, high) + dot(chosen, low)
                if i == 0 and extra:
                    out[count:, 0:rows] = refs[0][...]

    def tall(i):
        return pieces[i][2] + (8 if i == 0 and extra else 0)

    def place_of(start, parts):
        return lambda k: (0, jnp.clip(k + first - start, 0, parts - 1))

    return pl.pallas_call(
        kernel,
        grid=(steps,),
        in_specs=[pl.BlockSpec((8, rows), lambda k: (0, 0)), pl.BlockSpec((rows, step), lambda k: (0, k + first))]
        + [pl.BlockSpec((8, rows), lambda k: (0, 0))] * len(extra),
        out_specs=[pl.BlockSpec((tall(i), step), place_of(p[3], p[4])) for i, p in enumerate(pieces)],
        out_shape=[jax.ShapeDtypeStruct((tall(i), p[4] * step), F32) for i, p in enumerate(pieces)],
        compiler_params=params(room),
        cost_estimate=BRIEF,
        name=name,
    )(ranks, amplitudes, *extra)


def own_rows(own, mate, integrals, after):
    slots, width = own.shape
    cap = slots // 2
    cols = integrals.shape[1] // 2
    step = width // EIGHTHS

    def kernel(own_ref, mate_ref, right_ref, *refs):
        own_out, mate_out = refs[-2:]

        @pl.when(pl.program_id(0) == 0)
        def _():
            own_out[...] = jnp.zeros_like(own_out)
            mate_out[...] = jnp.zeros_like(mate_out)

        for j in range(2):
            at = slice(j * cap, (j + 1) * cap)
            left = jnp.concatenate([own_ref[at], mate_ref[at]], 0)
            both = product(left, right_ref[:, j * cols : (j + 1) * cols])
            own_out[at] += both[:cap]
            mate_out[at] += both[cap:]

    rows_spec = pl.BlockSpec((slots, step), lambda k: (0, k))
    out_spec = pl.BlockSpec((slots, cols), lambda k: (0, 0))
    out = jax.ShapeDtypeStruct((slots, cols), F32)
    return pl.pallas_call(
        kernel,
        grid=(width // step,),
        in_specs=[rows_spec, rows_spec, pl.BlockSpec((step, 2 * cols), lambda k: (k, 0))]
        + [pl.BlockSpec(memory_space=pl.ANY)] * len(after),
        out_specs=[out_spec, out_spec],
        out_shape=[out, out],
        compiler_params=params(32),
        cost_estimate=BRIEF,
        name="own_rows",
    )(own, mate, integrals, *after)


def crossed_rows(place, labels, cap, offset, own, mate, integrals, start, totals, final):
    taller = own.shape[0]
    count, width = min(taller, BLOCK) if offset == 0 else taller, own.shape[1]
    cols = integrals.shape[1] // 2
    step = integrals.shape[0] // EIGHTHS
    ranks = 4 * cap
    tile = min(512, cols)
    per = cols // tile
    slotted = count > cap
    tall = cap if slotted else count
    held = 2 * cap if slotted else count
    earlier = [] if totals is None else list(totals)
    sorted_out = slotted and final

    def kernel(place_ref, labels_own_ref, labels_mate_ref, own_ref, mate_ref, right_ref, *refs):
        before = refs[: len(earlier)]
        outs = refs[len(earlier) : len(earlier) + 2]
        left_ref = refs[len(earlier) + 2]
        sums = refs[len(earlier) + 3 :] if sorted_out else outs

        @pl.when(pl.program_id(0) == 0)
        def _():
            for i in range(2):
                sums[i][...] = before[i][...] if before else jnp.zeros_like(sums[i])

        wanted = lax.broadcasted_iota(jnp.int32, (count, ranks), 0) + offset
        at = lax.broadcasted_iota(jnp.int32, (count, ranks), 1)
        first_irrep = (4 * place_ref[0] + 2 * place_ref[1]).astype(F32)
        label_c = [jnp.sum(jnp.where(wanted == at, r[0:1, :], 0.0), axis=1, keepdims=True) for r in (labels_own_ref, labels_mate_ref)]
        values = (own_ref[...], mate_ref[...])
        if slotted:
            down = lax.broadcasted_iota(jnp.int32, (count, count), 0)
            across = lax.broadcasted_iota(jnp.int32, (count, count), 1)
            label_r = [jnp.sum(jnp.where(down == across, c, 0.0), axis=0, keepdims=True) for c in label_c]
            rank_r = [
                jnp.sum(jnp.where((down < across) & (c == r), 1.0, 0.0), axis=0, keepdims=True) for c, r in zip(label_c, label_r)
            ]
            slot = lax.broadcasted_iota(jnp.int32, (cap, count), 0).astype(F32)
            parts = [halves(v) for v in values]
            for j in range(2):
                irrep = first_irrep + float(j)
                chosen = [jnp.where((r == irrep) & (k == slot), 1.0, 0.0).astype(BF16) for r, k in zip(label_r, rank_r)]
                for h in range(2):
                    for p in range(2):
                        to = (2 * h + p) * cap
                        left_ref[j, to : to + cap] = dot(chosen[p], parts[p][h]).astype(BF16)
        else:
            label = jnp.concatenate(label_c, 0)
            value = jnp.concatenate(values, 0)
            for j in range(2):
                left_ref[j] = jnp.concatenate(halves(jnp.where(label == first_irrep + float(j), value, 0.0)), 0)

        def column(t, _):
            j = t // per
            high, low = halves(right_ref[:, pl.ds(pl.multiple_of(t * tile, tile), tile)])
            both = dot(left_ref[j], high)
            both = both[: 2 * tall] + both[2 * tall :] + dot(left_ref[j, : 2 * tall], low)
            to = pl.ds(pl.multiple_of((t % per) * tile, tile), tile)
            rows = pl.ds(pl.multiple_of(j * cap, cap), cap) if slotted else slice(None)
            sums[0][rows, to] += both[:tall]
            sums[1][rows, to] += both[tall:]
            return 0

        lax.fori_loop(0, 2 * per, column, 0)

        if sorted_out:

            @pl.when(pl.program_id(0) == pl.num_programs(0) - 1)
            def _():
                slot = lax.broadcasted_iota(jnp.int32, (count, cap), 1).astype(F32)
                for p in range(2):
                    rank_c = jnp.sum(
                        jnp.where((across < down) & (label_c[p] == label_r[p]), 1.0, 0.0), axis=1, keepdims=True
                    )
                    chosen = [
                        jnp.where((label_c[p] == first_irrep + float(j)) & (rank_c == slot), 1.0, 0.0).astype(BF16) for j in range(2)
                    ]
                    chosen = jnp.concatenate(chosen, 1)

                    def back(t, _):
                        to = pl.ds(pl.multiple_of(t * 256, 256), 256)
                        outs[p][:, to] = pick(chosen, sums[p][:, to])
                        return 0

                    lax.fori_loop(0, cols // 256, back, 0)

    label_spec = pl.BlockSpec((8, ranks), lambda k: (BLOCK // 8, 0))
    rows_spec = pl.BlockSpec((count, step), lambda k: (0, k))
    held_spec = pl.BlockSpec((held, cols), lambda k: (0, 0))
    given = count if final else held
    out_spec = pl.BlockSpec((given, cols), lambda k: (0, 0))
    return pl.pallas_call(
        kernel,
        grid=(width // step,),
        in_specs=[scalar(), label_spec, label_spec, rows_spec, rows_spec]
        + [pl.BlockSpec((step, 2 * cols), lambda k: (k + start, 0))]
        + [held_spec] * len(earlier),
        out_specs=[out_spec] * 2,
        out_shape=[jax.ShapeDtypeStruct((given, cols), F32)] * 2,
        scratch_shapes=[pltpu.VMEM((2, 4 * tall, step), BF16)] + [pltpu.VMEM((held, cols), F32)] * (2 if sorted_out else 0),
        compiler_params=params(32),
        cost_estimate=BRIEF,
        name="crossed_rows",
    )(place, *labels, own, mate, integrals, *earlier)


def spread(place, own, other, devices, stacked=False):
    rows, cols = own.shape
    block = cols // devices
    tall = 2 * rows if stacked else rows

    def kernel(place_ref, own_ref, other_ref, *outs):
        for m, out in enumerate(outs):
            at = pl.ds(pl.multiple_of((place_ref[2] ^ m) * block, block), block)
            if stacked:
                out[:rows] = own_ref[:, at]
                out[rows:] = other_ref[:, at]
            else:
                out[...] = own_ref[:, at] + other_ref[:, at]

    return pl.pallas_call(
        kernel,
        in_specs=[scalar(), whole(), whole()],
        out_specs=[whole()] * devices,
        out_shape=[jax.ShapeDtypeStruct((tall, block), F32)] * devices,
        compiler_params=params(16),
        cost_estimate=BRIEF,
        name="spread",
    )(place, own, other)


def assemble(place, columns, blocks):
    rows = columns.shape[0]
    devices = len(blocks[0][2])
    width = blocks[0][2][0].shape[1]

    counts = [arrays[0].shape[0] for _, _, arrays in blocks]
    starts = starts_of(counts)

    def kernel(place_ref, columns_ref, *refs):
        out, value_ref = refs[-2:]

        def chooser(kind, offset, count):
            wanted = lax.broadcasted_iota(jnp.int32, (rows, count), 1).astype(F32) + float(offset)
            return jnp.where(columns_ref[:, kind : kind + 1] == wanted, 1.0, 0.0).astype(BF16)

        for b, (start, count) in enumerate(zip(starts, counts)):
            for m in range(devices):
                value_ref[m, start : start + count] = refs[b * devices + m][...]
        chosen = [chooser(kind, offset, count) for (kind, offset, _), count in zip(blocks, counts)]

        def column(m, _):
            at = pl.ds(pl.multiple_of((place_ref[2] ^ m) * width, width), width)
            total = jnp.zeros((rows, width), F32)
            for part, start, count in zip(chosen, starts, counts):
                total = total + pick(part, value_ref[m, start : start + count])
            out[:, at] = total
            return 0

        lax.fori_loop(0, devices, column, 0)

    return pl.pallas_call(
        kernel,
        in_specs=[scalar(), whole()] + [whole()] * (devices * len(blocks)),
        out_specs=whole(),
        out_shape=jax.ShapeDtypeStruct((rows, width * devices), F32),
        scratch_shapes=[pltpu.VMEM((devices, sum(counts), width), F32)],
        compiler_params=params(16),
        cost_estimate=BRIEF,
        name="assemble",
    )(place, columns, *[a for _, _, arrays in blocks for a in arrays])


def swap_y(value, turn=0):
    return lax.ppermute(value, "redist", [(r, r ^ 2) for r in (*range(turn, 4), *range(turn))])


def swap_core(value):
    return lax.ppermute(value, "redist", [(r, r ^ 1) for r in range(4)])


def swap_z(value, m, devices):
    return lax.ppermute(value, "contract", [(z, z ^ m) for z in range(devices)])


def most_of(count):
    groups = lax.axis_size("groups")
    most = count
    for g in range(groups):
        for c in range(2):
            if g or c:
                pairs = [(4 * a + r, 4 * ((a + g) % groups) + (r ^ c)) for a in range(groups) for r in range(4)]
                most = jnp.maximum(most, lax.ppermute(count, ("groups", "redist"), pairs))
    return most


def home(value, m, devices):
    pairs = [(r * devices + z, (r ^ 2) * devices + (z ^ m)) for r in range(4) for z in range(devices)]
    return lax.ppermute(value, ("redist", "contract"), pairs)


def sum_z(blocks, devices):
    total = blocks[0]
    for m in range(1, devices):
        total = total + swap_z(blocks[m], m, devices)
    return total


def reduce_z(place, own, mate, devices):
    return sum_z(spread(place, own, swap_core(mate), devices), devices)


def gather_z(quarter, devices):
    return [quarter] + [swap_z(quarter, m, devices) for m in range(1, devices)]


def join(value, *others):
    return lax.optimization_barrier((value, *others))[0]


def rest(total, spare, integrals, place, columns, labels, block_own, block_totals, kept, devices, cap):
    rows = [swap_y(a[:total], i + 1) for i, a in enumerate(spare)]
    start = starts_of(BLOCK_PARTS)[1]
    totals = crossed_rows(place, labels, cap, 0, block_own, swap_core(block_own), integrals, start, block_totals, True)
    kept = gather_z(kept, devices)
    back = gather_z(swap_y(reduce_z(place, *totals, devices)), devices)

    totals, before = None, totals
    for i, (start, chunk) in enumerate(zip(starts_of(SPARE_PARTS), rows)):
        chunk = join(chunk, before[0], *kept[i + 1 : i + 2])
        final = i + 1 == len(rows)
        totals = crossed_rows(place, labels, cap, BLOCK, chunk, swap_core(chunk), integrals, start, totals, final)
        before = totals
    quarter = reduce_z(place, *totals, devices)
    last = [home(quarter, m, devices) for m in range(devices)]
    return assemble(place, columns, [(1, 0, kept), (0, 0, back), (0, BLOCK, last)])


def paired(amplitudes, pair_irrep, integrals):
    devices = lax.axis_size("contract")
    rows = amplitudes.shape[0]
    cap = rows // 4
    position = lax.axis_index("redist")
    place = jnp.stack([position // 2, position % 2, lax.axis_index("contract")]).astype(jnp.int32)
    ranks, columns, message = ranks_of(pair_irrep, place, cap)

    pieces = [(0, 0, BLOCK, 0, BLOCK_PARTS[0]), (1, 0, 2 * cap, 0, EIGHTHS), (1, 2 * cap, 2 * cap, 0, EIGHTHS)]
    sent, slots_own, slots_mate = pack(amplitudes, ranks, message, pieces, 56, "pack_first")
    first_own = swap_y(sent)
    own, mate = own_rows(slots_own, swap_core(slots_mate), integrals, (sent,))

    spare_rows = rows - BLOCK
    pieces = [(0, 0, BLOCK, BLOCK_PARTS[0], BLOCK_PARTS[1])]
    pieces += [(0, BLOCK, spare_rows, s, p) for s, p in zip(starts_of(SPARE_PARTS), SPARE_PARTS)]
    second, *spare = pack(amplitudes, join(ranks, own), None, pieces, 56, "pack_second")
    second_own = swap_y(second, 1)
    kept = spread(place, own, swap_core(mate), devices, stacked=True)

    first_own = join(first_own, second, *kept)
    first_mate = swap_core(first_own)
    labels = (first_own, first_mate)
    most = most_of(jnp.maximum(message[1:2, 0:128], first_own[BLOCK + 1 : BLOCK + 2, 0:128]))
    classes = [c for c in CLASSES if c < spare_rows] + [spare_rows]
    at = jnp.sum(jnp.asarray(classes, F32) + BLOCK < most[0, 0]).astype(jnp.int32)

    totals = crossed_rows(place, labels, cap, 0, first_own, first_mate, integrals, 0, None, False)
    kept = sum_z(kept, devices)
    branches = [functools.partial(rest, c, devices=devices, cap=cap) for c in classes]
    return lax.switch(at, branches, spare, integrals, place, columns, labels, second_own, totals, kept)


def general(amplitudes, pair_irrep, integrals):
    redist_count = lax.axis_size("redist")
    irreps_here = max(1, IRREPS // redist_count)
    copies = max(1, redist_count // IRREPS)
    pair_rows, contract_width = amplitudes.shape
    capacity = pair_rows // 4
    block_cols = integrals.shape[1] // irreps_here
    labels = pair_irrep[:, 0]
    onehot = (labels[:, None] == jnp.arange(IRREPS, dtype=jnp.int32)[None, :]).astype(jnp.int32)
    rank_in = jnp.sum(jnp.cumsum(onehot, axis=0) * onehot, axis=1) - 1
    slot_of = labels * capacity + rank_in
    source_rows = (
        jnp.full((IRREPS * capacity,), pair_rows, jnp.int32).at[slot_of].set(jnp.arange(pair_rows, dtype=jnp.int32))
    )
    source_rows = jnp.repeat(source_rows.reshape(IRREPS, 1, capacity), copies, axis=1).reshape(-1)
    gathered = jnp.take(amplitudes, source_rows, axis=0, mode="fill", fill_value=0.0)
    outgoing = gathered.reshape(redist_count, irreps_here, capacity, contract_width)
    local_cols = integrals.reshape(contract_width, irreps_here, block_cols)
    partial_value = jnp.einsum(
        "risk,kiw->risw",
        lax.all_to_all(outgoing, "redist", split_axis=0, concat_axis=0, tiled=True),
        local_cols,
        precision=lax.Precision.HIGHEST,
        preferred_element_type=F32,
    )
    summed = lax.psum(partial_value, "contract")
    returned = lax.all_to_all(summed, "redist", split_axis=0, concat_axis=0, tiled=True)
    by_irrep = returned.reshape(IRREPS, copies, capacity, block_cols)
    return by_irrep[labels, :, rank_in].reshape(pair_rows, copies * block_cols)


def shards(amplitudes, pair_irrep, integrals):
    rows, width = amplitudes.shape
    devices = lax.axis_size("contract")
    cols = integrals.shape[1] // 2
    fits = lax.axis_size("redist") == 4 and devices in (2, 4) and rows % 64 == 0 and rows > BLOCK
    if fits and width % (128 * EIGHTHS) == 0 and width >= rows * EIGHTHS and cols % (128 * devices) == 0:
        return paired(amplitudes, pair_irrep, integrals)
    return general(amplitudes, pair_irrep, integrals)


def solution(mesh):
    return jax.shard_map(
        shards,
        mesh=mesh,
        in_specs=(
            P(("groups", "redist"), "contract"),
            P(("groups", "redist"), None),
            P("contract", "redist"),
        ),
        out_specs=P(("groups", "redist"), None),
        check_vma=False,
    )
```

```python
import functools

import jax
import jax.numpy as jnp
from jax import lax
from jax.experimental import pallas as pl
from jax.experimental.pallas import tpu as pltpu
from jax.sharding import PartitionSpec as P

IRREPS = 8
F32 = jnp.float32
BF16 = jnp.bfloat16

CLASSES = (144, 160, 176, 192)
EIGHTHS = 8
PARTS = (5, 2, 1)
RING = 4

BRIEF = pl.CostEstimate(flops=1, bytes_accessed=1, transcendentals=0)

dot = functools.partial(jnp.dot, preferred_element_type=F32)


def halves(value):
    high = value.astype(BF16)
    return high, (value - high.astype(F32)).astype(BF16)


def thirds(value):
    high = value.astype(BF16)
    rest = value - high.astype(F32)
    middle = rest.astype(BF16)
    return high, middle, (rest - middle.astype(F32)).astype(BF16)


def product(left, right):
    rows = left.shape[0]
    left_high, left_low = halves(left)
    right_high, right_low = halves(right)
    both = dot(jnp.concatenate([left_high, left_low], 0), right_high)
    return both[:rows] + both[rows:] + dot(left_high, right_low)


def pick(chosen, value):
    high, middle, low = thirds(value)
    return dot(chosen, high) + dot(chosen, middle) + dot(chosen, low)


def starts_of(parts):
    return [sum(parts[:i]) for i in range(len(parts))]


def params(mebibytes):
    return pltpu.CompilerParams(vmem_limit_bytes=mebibytes << 20)


def whole():
    return pl.BlockSpec(memory_space=pltpu.VMEM)


def scalar():
    return pl.BlockSpec(memory_space=pltpu.SMEM)


def ranks_of(labels, place, cap):
    rows = labels.shape[0]

    def kernel(place_ref, labels_ref, row_ref, col_ref, message_ref):
        base = (4 * place_ref[0]).astype(F32)
        core = place_ref[1].astype(F32)
        down = lax.broadcasted_iota(jnp.int32, (rows, rows), 0)
        across = lax.broadcasted_iota(jnp.int32, (rows, rows), 1)
        label_c = labels_ref[...].astype(F32)
        label_r = jnp.sum(jnp.where(down == across, label_c, 0.0), axis=0, keepdims=True)

        def facts(label):
            local = label - base
            stays = (local >= 0) & (local < 4)
            owner = jnp.where(local >= 2, 1.0, 0.0)
            order = jnp.where(owner == core, 0.0, 2.0) + (local - 2 * owner)
            return stays, order * cap

        stays_c, slot_c = facts(label_c)
        stays_r, slot_r = facts(label_r)
        cross_c = jnp.where(stays_c, 0.0, 1.0)
        cross_r = jnp.where(stays_r, 0.0, 1.0)
        alike = jnp.where(label_c == label_r, 1.0, 0.0)
        ahead = down < across
        rank_r = jnp.sum(jnp.where(ahead, cross_c, 0.0), axis=0, keepdims=True)
        rank_c = jnp.sum(jnp.where(across < down, cross_r, 0.0), axis=1, keepdims=True)
        inner_r = jnp.sum(jnp.where(ahead, alike, 0.0), axis=0, keepdims=True)
        inner_c = jnp.sum(jnp.where(across < down, alike, 0.0), axis=1, keepdims=True)
        rank_r = jnp.where(stays_r, -1.0, rank_r)
        rank_c = jnp.where(stays_c, -1.0, rank_c)
        slot_r = jnp.where(stays_r, slot_r + inner_r, -1.0)
        slot_c = jnp.where(stays_c, slot_c + inner_c, -1.0)
        sub = lax.broadcasted_iota(jnp.int32, (8, rows), 0)
        row_ref[...] = jnp.where(sub == 0, rank_r, slot_r)
        lane = lax.broadcasted_iota(jnp.int32, (rows, 128), 1)
        col_ref[...] = jnp.where(lane == 0, rank_c, slot_c)
        sent = jnp.sum(jnp.where(rank_c == across.astype(F32), label_c + 1.0, 0.0), axis=0, keepdims=True) - 1.0
        count = jnp.sum(cross_r, axis=1, keepdims=True)
        message_ref[...] = jnp.where(sub == 0, sent, count)

    return pl.pallas_call(
        kernel,
        in_specs=[scalar(), whole()],
        out_specs=[whole()] * 3,
        out_shape=[
            jax.ShapeDtypeStruct((8, rows), F32),
            jax.ShapeDtypeStruct((rows, 128), F32),
            jax.ShapeDtypeStruct((8, rows), F32),
        ],
        compiler_params=params(16),
        name="ranks",
    )(place, labels)


def pack(amplitudes, ranks, pieces, name):
    rows, width = amplitudes.shape
    step = width // EIGHTHS
    cuts = sorted({p[3] for p in pieces} | {p[3] + p[4] for p in pieces})

    def kernel(ranks_ref, value_ref, *outs):
        for low_cut, high_cut in zip(cuts, cuts[1:]):
            active = [(p, out) for p, out in zip(pieces, outs) if p[3] <= low_cut < p[3] + p[4]]
            if not active:
                continue
            chosen = []
            for (kind, offset, count, _, _), _ in active:
                wanted = lax.broadcasted_iota(jnp.int32, (count, rows), 0).astype(F32) + float(offset)
                chosen.append(jnp.where(ranks_ref[kind : kind + 1, :] == wanted, 1.0, 0.0).astype(BF16))
            chosen = jnp.concatenate(chosen, 0)

            def column(k, _):
                high, low = halves(value_ref[:, pl.ds(pl.multiple_of(k * step, step), step)])
                found = dot(chosen, high) + dot(chosen, low)
                at = 0
                for (_, _, count, start, _), out in active:
                    out[0:count, pl.ds(pl.multiple_of((k - start) * step, step), step)] = found[at : at + count]
                    at += count
                return 0

            lax.fori_loop(low_cut, high_cut, column, 0)

    return pl.pallas_call(
        kernel,
        in_specs=[whole()] * 2,
        out_specs=[whole()] * len(pieces),
        out_shape=[jax.ShapeDtypeStruct((p[2], p[4] * step), F32) for p in pieces],
        compiler_params=params(16),
        cost_estimate=BRIEF,
        name=name,
    )(ranks, amplitudes)


def own_rows(place, own, mate, integrals):
    slots, width = own.shape
    cap = slots // 2
    cols = integrals.shape[1] // 2
    block = cols // RING
    step = width // EIGHTHS
    tile = min(512, cols)
    per = cols // tile

    def kernel(place_ref, own_ref, mate_ref, right_ref, *refs):
        outs, sum_ref, left_ref = refs[:RING], refs[RING], refs[RING + 1]

        @pl.when(pl.program_id(0) == 0)
        def _():
            sum_ref[...] = jnp.zeros_like(sum_ref)

        for j in range(2):
            at = slice(j * cap, (j + 1) * cap)
            left_ref[j] = jnp.concatenate(halves(jnp.concatenate([own_ref[at], mate_ref[at]], 0)), 0)

        def column(t, _):
            j = t // per
            high, low = halves(right_ref[:, pl.ds(pl.multiple_of(t * tile, tile), tile)])
            both = dot(left_ref[j], high)
            both = both[:slots] + both[slots:] + dot(left_ref[j, :slots], low)
            to = pl.ds(pl.multiple_of((t % per) * tile, tile), tile)
            sum_ref[pl.ds(pl.multiple_of(j * cap, cap), cap), to] += both[:cap]
            sum_ref[pl.ds(pl.multiple_of(slots + j * cap, cap), cap), to] += both[cap:]
            return 0

        lax.fori_loop(0, 2 * per, column, 0)

        @pl.when(pl.program_id(0) == pl.num_programs(0) - 1)
        def _():
            for m, out in enumerate(outs):
                out[...] = sum_ref[:, pl.ds(pl.multiple_of((place_ref[2] ^ m) * block, block), block)]

    rows_spec = pl.BlockSpec((slots, step), lambda k: (0, k))
    return pl.pallas_call(
        kernel,
        grid=(EIGHTHS,),
        in_specs=[scalar(), rows_spec, rows_spec, pl.BlockSpec((step, 2 * cols), lambda k: (k, 0))],
        out_specs=[pl.BlockSpec((2 * slots, block), lambda k: (0, 0))] * RING,
        out_shape=[jax.ShapeDtypeStruct((2 * slots, block), F32)] * RING,
        scratch_shapes=[pltpu.VMEM((2 * slots, cols), F32), pltpu.VMEM((2, 2 * slots, step), BF16)],
        compiler_params=params(32),
        cost_estimate=BRIEF,
        name="own_rows",
    )(place, own, mate, integrals)


def crossed_rows(place, labels, cap, own, mate, integrals, start, totals, final):
    count, width = own.shape
    cols = integrals.shape[1] // 2
    step = integrals.shape[0] // EIGHTHS
    ranks = 4 * cap
    tile = min(512, cols)
    per = cols // tile
    slotted = count > cap
    tall = cap if slotted else count
    held = 2 * cap if slotted else count
    earlier = [] if totals is None else list(totals)
    sorted_out = slotted and final

    def kernel(place_ref, labels_own_ref, labels_mate_ref, own_ref, mate_ref, right_ref, *refs):
        before = refs[: len(earlier)]
        outs = refs[len(earlier) : len(earlier) + 2]
        left_ref = refs[len(earlier) + 2]
        sums = refs[len(earlier) + 3 :] if sorted_out else outs

        @pl.when(pl.program_id(0) == 0)
        def _():
            for i in range(2):
                sums[i][...] = before[i][...] if before else jnp.zeros_like(sums[i])

        wanted = lax.broadcasted_iota(jnp.int32, (count, ranks), 0)
        at = lax.broadcasted_iota(jnp.int32, (count, ranks), 1)
        first_irrep = (4 * place_ref[0] + 2 * place_ref[1]).astype(F32)
        label_c = [jnp.sum(jnp.where(wanted == at, r[0:1, :], 0.0), axis=1, keepdims=True) for r in (labels_own_ref, labels_mate_ref)]
        values = (own_ref[...], mate_ref[...])
        if slotted:
            down = lax.broadcasted_iota(jnp.int32, (count, count), 0)
            across = lax.broadcasted_iota(jnp.int32, (count, count), 1)
            label_r = [jnp.sum(jnp.where(down == across, c, 0.0), axis=0, keepdims=True) for c in label_c]
            rank_r = [
                jnp.sum(jnp.where((down < across) & (c == r), 1.0, 0.0), axis=0, keepdims=True) for c, r in zip(label_c, label_r)
            ]
            slot = lax.broadcasted_iota(jnp.int32, (cap, count), 0).astype(F32)
            parts = [halves(v) for v in values]
            for j in range(2):
                irrep = first_irrep + float(j)
                chosen = [jnp.where((r == irrep) & (k == slot), 1.0, 0.0).astype(BF16) for r, k in zip(label_r, rank_r)]
                for h in range(2):
                    for p in range(2):
                        to = (2 * h + p) * cap
                        left_ref[j, to : to + cap] = dot(chosen[p], parts[p][h]).astype(BF16)
        else:
            label = jnp.concatenate(label_c, 0)
            value = jnp.concatenate(values, 0)
            for j in range(2):
                left_ref[j] = jnp.concatenate(halves(jnp.where(label == first_irrep + float(j), value, 0.0)), 0)

        def column(t, _):
            j = t // per
            high, low = halves(right_ref[:, pl.ds(pl.multiple_of(t * tile, tile), tile)])
            both = dot(left_ref[j], high)
            both = both[: 2 * tall] + both[2 * tall :] + dot(left_ref[j, : 2 * tall], low)
            to = pl.ds(pl.multiple_of((t % per) * tile, tile), tile)
            rows = pl.ds(pl.multiple_of(j * cap, cap), cap) if slotted else slice(None)
            sums[0][rows, to] += both[:tall]
            sums[1][rows, to] += both[tall:]
            return 0

        lax.fori_loop(0, 2 * per, column, 0)

        if sorted_out:

            @pl.when(pl.program_id(0) == pl.num_programs(0) - 1)
            def _():
                slot = lax.broadcasted_iota(jnp.int32, (count, cap), 1).astype(F32)
                for p in range(2):
                    rank_c = jnp.sum(
                        jnp.where((across < down) & (label_c[p] == label_r[p]), 1.0, 0.0), axis=1, keepdims=True
                    )
                    chosen = [
                        jnp.where((label_c[p] == first_irrep + float(j)) & (rank_c == slot), 1.0, 0.0).astype(BF16) for j in range(2)
                    ]
                    chosen = jnp.concatenate(chosen, 1)

                    def back(t, _):
                        to = pl.ds(pl.multiple_of(t * 256, 256), 256)
                        outs[p][:, to] = pick(chosen, sums[p][:, to])
                        return 0

                    lax.fori_loop(0, cols // 256, back, 0)

    label_spec = pl.BlockSpec((8, ranks), lambda k: (0, 0))
    rows_spec = pl.BlockSpec((count, step), lambda k: (0, k))
    held_spec = pl.BlockSpec((held, cols), lambda k: (0, 0))
    given = count if final else held
    out_spec = pl.BlockSpec((given, cols), lambda k: (0, 0))
    return pl.pallas_call(
        kernel,
        grid=(width // step,),
        in_specs=[scalar(), label_spec, label_spec, rows_spec, rows_spec]
        + [pl.BlockSpec((step, 2 * cols), lambda k: (k + start, 0))]
        + [held_spec] * len(earlier),
        out_specs=[out_spec] * 2,
        out_shape=[jax.ShapeDtypeStruct((given, cols), F32)] * 2,
        scratch_shapes=[pltpu.VMEM((2, 4 * tall, step), BF16)] + [pltpu.VMEM((held, cols), F32)] * (2 if sorted_out else 0),
        compiler_params=params(32),
        cost_estimate=BRIEF,
        name="crossed_rows",
    )(place, *labels, own, mate, integrals, *earlier)


def spread(place, own, other, devices, stacked=False):
    rows, cols = own.shape
    block = cols // devices
    tall = 2 * rows if stacked else rows

    def kernel(place_ref, own_ref, other_ref, *outs):
        for m, out in enumerate(outs):
            at = pl.ds(pl.multiple_of((place_ref[2] ^ m) * block, block), block)
            if stacked:
                out[:rows] = own_ref[:, at]
                out[rows:] = other_ref[:, at]
            else:
                out[...] = own_ref[:, at] + other_ref[:, at]

    return pl.pallas_call(
        kernel,
        in_specs=[scalar(), whole(), whole()],
        out_specs=[whole()] * devices,
        out_shape=[jax.ShapeDtypeStruct((tall, block), F32)] * devices,
        compiler_params=params(16),
        cost_estimate=BRIEF,
        name="spread",
    )(place, own, other)


def assemble(place, columns, blocks):
    rows = columns.shape[0]
    devices = len(blocks[0][2])
    width = blocks[0][2][0].shape[1]

    counts = [arrays[0].shape[0] for _, _, arrays in blocks]
    starts = starts_of(counts)

    def kernel(place_ref, columns_ref, *refs):
        out, value_ref, chosen_ref = refs[-3:]

        def chooser(kind, offset, count):
            wanted = lax.broadcasted_iota(jnp.int32, (rows, count), 1).astype(F32) + float(offset)
            return jnp.where(columns_ref[:, kind : kind + 1] == wanted, 1.0, 0.0).astype(BF16)

        for b, (start, count) in enumerate(zip(starts, counts)):
            for m in range(devices):
                value_ref[m, start : start + count] = refs[b * devices + m][...]
            chosen_ref[:, start : start + count] = chooser(blocks[b][0], blocks[b][1], count)

        def column(t, _):
            m, half = t // 2, pl.multiple_of(t % 2 * (rows // 2), rows // 2)
            at = pl.ds(pl.multiple_of((place_ref[2] ^ m) * width, width), width)
            out[pl.ds(half, rows // 2), at] = pick(chosen_ref[pl.ds(half, rows // 2)], value_ref[m])
            return 0

        lax.fori_loop(0, 2 * devices, column, 0)

    return pl.pallas_call(
        kernel,
        in_specs=[scalar(), whole()] + [whole()] * (devices * len(blocks)),
        out_specs=whole(),
        out_shape=jax.ShapeDtypeStruct((rows, width * devices), F32),
        scratch_shapes=[pltpu.VMEM((devices, sum(counts), width), F32), pltpu.VMEM((rows, sum(counts)), BF16)],
        compiler_params=params(16),
        cost_estimate=BRIEF,
        name="assemble",
    )(place, columns, *[a for _, _, arrays in blocks for a in arrays])


def swap_y(value, turn=0):
    return lax.ppermute(value, "redist", [(r, r ^ 2) for r in (*range(turn, 4), *range(turn))])


def swap_core(value):
    return lax.ppermute(value, "redist", [(r, r ^ 1) for r in range(4)])


def swap_z(value, m, devices):
    return lax.ppermute(value, "contract", [(z, z ^ m) for z in range(devices)])


def most_of(count):
    groups = lax.axis_size("groups")
    most = count
    for g in range(groups):
        for c in range(2):
            if g or c:
                pairs = [(4 * a + r, 4 * ((a + g) % groups) + (r ^ c)) for a in range(groups) for r in range(4)]
                most = jnp.maximum(most, lax.ppermute(count, ("groups", "redist"), pairs))
    return most


def home(value, m, devices):
    pairs = [(r * devices + z, (r ^ 2) * devices + (z ^ m)) for r in range(4) for z in range(devices)]
    return lax.ppermute(value, ("redist", "contract"), pairs)


def sum_z(blocks, devices):
    total = blocks[0]
    for m in range(1, devices):
        total = total + swap_z(blocks[m], m, devices)
    return total


def reduce_z(place, own, mate, devices):
    return sum_z(spread(place, own, swap_core(mate), devices), devices)


def gather_z(quarter, devices):
    return [quarter] + [swap_z(quarter, m, devices) for m in range(1, devices)]


def join(value, *others):
    return lax.optimization_barrier((value, *others))[0]


def crossing(total, spare, slots_own, slots_mate, integrals, place, columns, labels, cap):
    rows = [swap_y(a[:total]) for a in spare]
    blocks = own_rows(place, slots_own, swap_core(slots_mate), integrals)
    reduced = sum_z(blocks, RING)
    quarter = jnp.concatenate([reduced[: 2 * cap], swap_core(reduced[2 * cap :])], 0)
    kept = gather_z(quarter, RING)

    ahead = [(quarter,), kept, ()]
    totals = None
    for i, (start, chunk) in enumerate(zip(starts_of(PARTS), rows)):
        chunk = join(chunk, *ahead[i], *(totals or ()))
        totals = crossed_rows(place, labels, cap, chunk, swap_core(chunk), integrals, start, totals, i + 1 == len(rows))
    quarter = reduce_z(place, *totals, RING)
    last = [home(quarter, m, RING) for m in range(RING)]
    return assemble(place, columns, [(1, 0, kept), (0, 0, last)])


def paired(amplitudes, pair_irrep, integrals):
    rows = amplitudes.shape[0]
    cap = rows // 4
    position = lax.axis_index("redist")
    place = jnp.stack([position // 2, position % 2, lax.axis_index("contract")]).astype(jnp.int32)
    ranks, columns, message = ranks_of(pair_irrep, place, cap)
    labels_own = swap_y(message)
    labels = (labels_own, swap_core(labels_own))
    pieces = [(1, 0, 2 * cap, 0, EIGHTHS), (1, 2 * cap, 2 * cap, 0, EIGHTHS)]
    pieces += [(0, 0, rows, start, parts) for start, parts in zip(starts_of(PARTS), PARTS)]
    slots_own, slots_mate, *spare = pack(amplitudes, ranks, pieces, "pack")
    most = most_of(jnp.maximum(message, labels_own)[1:2, 0:128])
    classes = [c for c in CLASSES if c < rows] + [rows]
    at = jnp.sum(jnp.asarray(classes, F32) < most[0, 0]).astype(jnp.int32)
    branches = [functools.partial(crossing, c, cap=cap) for c in classes]
    return lax.switch(at, branches, spare, slots_own, slots_mate, integrals, place, columns, labels)


def general(amplitudes, pair_irrep, integrals):
    redist_count = lax.axis_size("redist")
    irreps_here = max(1, IRREPS // redist_count)
    copies = max(1, redist_count // IRREPS)
    pair_rows, contract_width = amplitudes.shape
    capacity = pair_rows // 4
    block_cols = integrals.shape[1] // irreps_here
    labels = pair_irrep[:, 0]
    onehot = (labels[:, None] == jnp.arange(IRREPS, dtype=jnp.int32)[None, :]).astype(jnp.int32)
    rank_in = jnp.sum(jnp.cumsum(onehot, axis=0) * onehot, axis=1) - 1
    slot_of = labels * capacity + rank_in
    source_rows = (
        jnp.full((IRREPS * capacity,), pair_rows, jnp.int32).at[slot_of].set(jnp.arange(pair_rows, dtype=jnp.int32))
    )
    source_rows = jnp.repeat(source_rows.reshape(IRREPS, 1, capacity), copies, axis=1).reshape(-1)
    gathered = jnp.take(amplitudes, source_rows, axis=0, mode="fill", fill_value=0.0)
    outgoing = gathered.reshape(redist_count, irreps_here, capacity, contract_width)
    local_cols = integrals.reshape(contract_width, irreps_here, block_cols)
    partial_value = jnp.einsum(
        "risk,kiw->risw",
        lax.all_to_all(outgoing, "redist", split_axis=0, concat_axis=0, tiled=True),
        local_cols,
        precision=lax.Precision.HIGHEST,
        preferred_element_type=F32,
    )
    summed = lax.psum(partial_value, "contract")
    returned = lax.all_to_all(summed, "redist", split_axis=0, concat_axis=0, tiled=True)
    by_irrep = returned.reshape(IRREPS, copies, capacity, block_cols)
    return by_irrep[labels, :, rank_in].reshape(pair_rows, copies * block_cols)


def shards(amplitudes, pair_irrep, integrals):
    rows, width = amplitudes.shape
    cols = integrals.shape[1] // 2
    fits = lax.axis_size("redist") == 4 and lax.axis_size("contract") == RING and rows % 64 == 0
    if fits and width % (128 * EIGHTHS) == 0 and cols % (256 * RING) == 0:
        return paired(amplitudes, pair_irrep, integrals)
    return general(amplitudes, pair_irrep, integrals)


def solution(mesh):
    return jax.shard_map(
        shards,
        mesh=mesh,
        in_specs=(
            P(("groups", "redist"), "contract"),
            P(("groups", "redist"), None),
            P("contract", "redist"),
        ),
        out_specs=P(("groups", "redist"), None),
        check_vma=False,
    )
```

```python
import functools

import jax
import jax.numpy as jnp
from jax import lax
from jax.experimental import pallas as pl
from jax.experimental.pallas import tpu as pltpu
from jax.sharding import PartitionSpec as P

IRREPS = 8
F32 = jnp.float32
BF16 = jnp.bfloat16

CLASSES = (152, 168, 184, 200)
EIGHTHS = 8
PARTS = (5, 2, 1)
RING = 4
FAR_FIRST = (2, 3, 1, 0)

BRIEF = pl.CostEstimate(flops=1, bytes_accessed=1, transcendentals=0)

dot = functools.partial(jnp.dot, preferred_element_type=F32)


def halves(value):
    high = value.astype(BF16)
    return high, (value - high.astype(F32)).astype(BF16)


def pick(chosen, value):
    high, low = halves(value)
    return dot(chosen, high) + dot(chosen, low)


def starts_of(parts):
    return [sum(parts[:i]) for i in range(len(parts))]


def params(mebibytes):
    return pltpu.CompilerParams(vmem_limit_bytes=mebibytes << 20)


def whole():
    return pl.BlockSpec(memory_space=pltpu.VMEM)


def scalar():
    return pl.BlockSpec(memory_space=pltpu.SMEM)


def ranks_of(labels, place, cap):
    rows = labels.shape[0]

    def kernel(place_ref, labels_ref, row_ref, col_ref, message_ref):
        base = (4 * place_ref[0]).astype(F32)
        core = place_ref[1].astype(F32)
        down = lax.broadcasted_iota(jnp.int32, (rows, rows), 0)
        across = lax.broadcasted_iota(jnp.int32, (rows, rows), 1)
        label_c = labels_ref[...].astype(F32)
        label_r = jnp.sum(jnp.where(down == across, label_c, 0.0), axis=0, keepdims=True)

        def facts(label):
            local = label - base
            stays = (local >= 0) & (local < 4)
            owner = jnp.where(local >= 2, 1.0, 0.0)
            order = jnp.where(owner == core, 0.0, 2.0) + (local - 2 * owner)
            return stays, order * cap

        stays_c, slot_c = facts(label_c)
        stays_r, slot_r = facts(label_r)
        cross_c = jnp.where(stays_c, 0.0, 1.0)
        cross_r = jnp.where(stays_r, 0.0, 1.0)
        alike = jnp.where(label_c == label_r, 1.0, 0.0)
        ahead = down < across
        rank_r = jnp.sum(jnp.where(ahead, cross_c, 0.0), axis=0, keepdims=True)
        rank_c = jnp.sum(jnp.where(across < down, cross_r, 0.0), axis=1, keepdims=True)
        inner_r = jnp.sum(jnp.where(ahead, alike, 0.0), axis=0, keepdims=True)
        inner_c = jnp.sum(jnp.where(across < down, alike, 0.0), axis=1, keepdims=True)
        rank_r = jnp.where(stays_r, -1.0, rank_r)
        rank_c = jnp.where(stays_c, -1.0, rank_c)
        slot_r = jnp.where(stays_r, slot_r + inner_r, -1.0)
        slot_c = jnp.where(stays_c, slot_c + inner_c, -1.0)
        sub = lax.broadcasted_iota(jnp.int32, (8, rows), 0)
        row_ref[...] = jnp.where(sub == 0, rank_r, slot_r)
        lane = lax.broadcasted_iota(jnp.int32, (rows, 128), 1)
        col_ref[...] = jnp.where(lane == 0, rank_c, slot_c)
        sent = jnp.sum(jnp.where(rank_c == across.astype(F32), label_c + 1.0, 0.0), axis=0, keepdims=True) - 1.0
        count = jnp.sum(cross_r, axis=1, keepdims=True)
        message_ref[...] = jnp.where(sub == 0, sent, count)

    return pl.pallas_call(
        kernel,
        in_specs=[scalar(), whole()],
        out_specs=[whole()] * 3,
        out_shape=[
            jax.ShapeDtypeStruct((8, rows), F32),
            jax.ShapeDtypeStruct((rows, 128), F32),
            jax.ShapeDtypeStruct((8, rows), F32),
        ],
        compiler_params=params(16),
        name="ranks",
    )(place, labels)


def pack(amplitudes, ranks, pieces, name):
    rows, width = amplitudes.shape
    step = width // EIGHTHS
    cuts = sorted({p[3] for p in pieces} | {p[3] + p[4] for p in pieces})

    def kernel(ranks_ref, value_ref, *outs):
        for low_cut, high_cut in zip(cuts, cuts[1:]):
            active = [(p, out) for p, out in zip(pieces, outs) if p[3] <= low_cut < p[3] + p[4]]
            if not active:
                continue
            chosen = []
            for (kind, offset, count, _, _), _ in active:
                wanted = lax.broadcasted_iota(jnp.int32, (count, rows), 0).astype(F32) + float(offset)
                chosen.append(jnp.where(ranks_ref[kind : kind + 1, :] == wanted, 1.0, 0.0).astype(BF16))
            chosen = jnp.concatenate(chosen, 0)

            def column(k, _):
                high, low = halves(value_ref[:, pl.ds(pl.multiple_of(k * step, step), step)])
                found = dot(chosen, high) + dot(chosen, low)
                at = 0
                for (_, _, count, start, _), out in active:
                    out[0:count, pl.ds(pl.multiple_of((k - start) * step, step), step)] = found[at : at + count]
                    at += count
                return 0

            lax.fori_loop(low_cut, high_cut, column, 0)

    return pl.pallas_call(
        kernel,
        in_specs=[whole()] * 2,
        out_specs=[whole()] * len(pieces),
        out_shape=[jax.ShapeDtypeStruct((p[2], p[4] * step), F32) for p in pieces],
        compiler_params=params(16),
        cost_estimate=BRIEF,
        name=name,
    )(ranks, amplitudes)


def own_rows(place, ranks_own, ranks_mate, own, mate, integrals, cap):
    rows, width = own.shape
    slots = 2 * cap
    cols = integrals.shape[1] // 2
    block = cols // RING
    step = width // EIGHTHS
    tile = min(512, cols)
    per = cols // tile

    def kernel(place_ref, ranks_own_ref, ranks_mate_ref, own_ref, mate_ref, right_ref, *refs):
        outs, sum_ref, left_ref = refs[:RING], refs[RING], refs[RING + 1]

        @pl.when(pl.program_id(0) == 0)
        def _():
            sum_ref[...] = jnp.zeros_like(sum_ref)

        for p, (ranks_ref, value_ref) in enumerate(((ranks_own_ref, own_ref), (ranks_mate_ref, mate_ref))):
            wanted = lax.broadcasted_iota(jnp.int32, (slots, rows), 0).astype(F32) + float(p * slots)
            chosen = jnp.where(ranks_ref[1:2, :] == wanted, 1.0, 0.0).astype(BF16)
            for h, part in enumerate(halves(value_ref[...])):
                found = dot(chosen, part).astype(BF16)
                to = (2 * h + p) * cap
                for j in range(2):
                    left_ref[j, to : to + cap] = found[j * cap : (j + 1) * cap]

        def column(t, _):
            j = t // per
            high, low = halves(right_ref[:, pl.ds(pl.multiple_of(t * tile, tile), tile)])
            both = dot(left_ref[j], high)
            both = both[:slots] + both[slots:] + dot(left_ref[j, :slots], low)
            to = pl.ds(pl.multiple_of((t % per) * tile, tile), tile)
            sum_ref[pl.ds(pl.multiple_of(j * cap, cap), cap), to] += both[:cap]
            sum_ref[pl.ds(pl.multiple_of(slots + j * cap, cap), cap), to] += both[cap:]
            return 0

        lax.fori_loop(0, 2 * per, column, 0)

        @pl.when(pl.program_id(0) == pl.num_programs(0) - 1)
        def _():
            for m, out in enumerate(outs):
                out[...] = sum_ref[:, pl.ds(pl.multiple_of((place_ref[2] ^ m) * block, block), block)]

    ranks_spec = pl.BlockSpec((8, rows), lambda k: (0, 0))
    rows_spec = pl.BlockSpec((rows, step), lambda k: (0, k))
    return pl.pallas_call(
        kernel,
        grid=(EIGHTHS,),
        in_specs=[scalar(), ranks_spec, ranks_spec, rows_spec, rows_spec, pl.BlockSpec((step, 2 * cols), lambda k: (k, 0))],
        out_specs=[pl.BlockSpec((2 * slots, block), lambda k: (0, 0))] * RING,
        out_shape=[jax.ShapeDtypeStruct((2 * slots, block), F32)] * RING,
        scratch_shapes=[pltpu.VMEM((2 * slots, cols), F32), pltpu.VMEM((2, 2 * slots, step), BF16)],
        compiler_params=params(32),
        cost_estimate=BRIEF,
        name="own_rows",
    )(place, ranks_own, ranks_mate, own, mate, integrals)


def crossed_rows(place, labels, cap, own, mate, integrals, start, totals, final):
    count, width = sum(a.shape[0] for a in own), own[0].shape[1]
    cols = integrals.shape[1] // 2
    step = integrals.shape[0] // EIGHTHS
    pieces = len(own)
    ranks = 4 * cap
    tile = min(512, cols)
    per = cols // tile
    slotted = count > cap
    tall = cap if slotted else count
    held = 2 * cap if slotted else count
    earlier = [] if totals is None else list(totals)
    sorted_out = slotted and final

    def kernel(place_ref, labels_own_ref, labels_mate_ref, *refs):
        values = [jnp.concatenate([r[...] for r in refs[p * pieces : (p + 1) * pieces]], 0) for p in range(2)]
        right_ref, *refs = refs[2 * pieces :]
        before = refs[: len(earlier)]
        outs = refs[len(earlier) : len(earlier) + 2]
        left_ref = refs[len(earlier) + 2]
        sums = refs[len(earlier) + 3 :] if sorted_out else outs

        @pl.when(pl.program_id(0) == 0)
        def _():
            for i in range(2):
                sums[i][...] = before[i][...] if before else jnp.zeros_like(sums[i])

        wanted = lax.broadcasted_iota(jnp.int32, (count, ranks), 0)
        at = lax.broadcasted_iota(jnp.int32, (count, ranks), 1)
        first_irrep = (4 * place_ref[0] + 2 * place_ref[1]).astype(F32)
        label_c = [jnp.sum(jnp.where(wanted == at, r[0:1, :], 0.0), axis=1, keepdims=True) for r in (labels_own_ref, labels_mate_ref)]
        if slotted:
            down = lax.broadcasted_iota(jnp.int32, (count, count), 0)
            across = lax.broadcasted_iota(jnp.int32, (count, count), 1)
            label_r = [jnp.sum(jnp.where(down == across, c, 0.0), axis=0, keepdims=True) for c in label_c]
            rank_r = [
                jnp.sum(jnp.where((down < across) & (c == r), 1.0, 0.0), axis=0, keepdims=True) for c, r in zip(label_c, label_r)
            ]
            slot = lax.broadcasted_iota(jnp.int32, (cap, count), 0).astype(F32)
            parts = [halves(v) for v in values]
            for j in range(2):
                irrep = first_irrep + float(j)
                chosen = [jnp.where((r == irrep) & (k == slot), 1.0, 0.0).astype(BF16) for r, k in zip(label_r, rank_r)]
                for h in range(2):
                    for p in range(2):
                        to = (2 * h + p) * cap
                        left_ref[j, to : to + cap] = dot(chosen[p], parts[p][h]).astype(BF16)
        else:
            label = jnp.concatenate(label_c, 0)
            value = jnp.concatenate(values, 0)
            for j in range(2):
                left_ref[j] = jnp.concatenate(halves(jnp.where(label == first_irrep + float(j), value, 0.0)), 0)

        def column(t, _):
            j = t // per
            high, low = halves(right_ref[:, pl.ds(pl.multiple_of(t * tile, tile), tile)])
            both = dot(left_ref[j], high)
            both = both[: 2 * tall] + both[2 * tall :] + dot(left_ref[j, : 2 * tall], low)
            to = pl.ds(pl.multiple_of((t % per) * tile, tile), tile)
            rows = pl.ds(pl.multiple_of(j * cap, cap), cap) if slotted else slice(None)
            sums[0][rows, to] += both[:tall]
            sums[1][rows, to] += both[tall:]
            return 0

        lax.fori_loop(0, 2 * per, column, 0)

        if sorted_out:

            @pl.when(pl.program_id(0) == pl.num_programs(0) - 1)
            def _():
                slot = lax.broadcasted_iota(jnp.int32, (count, cap), 1).astype(F32)
                for p in range(2):
                    rank_c = jnp.sum(
                        jnp.where((across < down) & (label_c[p] == label_r[p]), 1.0, 0.0), axis=1, keepdims=True
                    )
                    chosen = [
                        jnp.where((label_c[p] == first_irrep + float(j)) & (rank_c == slot), 1.0, 0.0).astype(BF16) for j in range(2)
                    ]
                    chosen = jnp.concatenate(chosen, 1)

                    def back(t, _):
                        to = pl.ds(pl.multiple_of(t * 256, 256), 256)
                        outs[p][:, to] = pick(chosen, sums[p][:, to])
                        return 0

                    lax.fori_loop(0, cols // 256, back, 0)

    label_spec = pl.BlockSpec((8, ranks), lambda k: (0, 0))
    held_spec = pl.BlockSpec((held, cols), lambda k: (0, 0))
    given = count if final else held
    out_spec = pl.BlockSpec((given, cols), lambda k: (0, 0))
    return pl.pallas_call(
        kernel,
        grid=(width // step,),
        in_specs=[scalar(), label_spec, label_spec]
        + [pl.BlockSpec((a.shape[0], step), lambda k: (0, k)) for a in own + mate]
        + [pl.BlockSpec((step, 2 * cols), lambda k: (k + start, 0))]
        + [held_spec] * len(earlier),
        out_specs=[out_spec] * 2,
        out_shape=[jax.ShapeDtypeStruct((given, cols), F32)] * 2,
        scratch_shapes=[pltpu.VMEM((2, 4 * tall, step), BF16)] + [pltpu.VMEM((held, cols), F32)] * (2 if sorted_out else 0),
        compiler_params=params(32),
        cost_estimate=BRIEF,
        name="crossed_rows",
    )(place, *labels, *own, *mate, integrals, *earlier)


def spread(place, own, other, devices, stacked=False):
    rows, cols = own.shape
    block = cols // devices
    tall = 2 * rows if stacked else rows

    def kernel(place_ref, own_ref, other_ref, *outs):
        for m, out in enumerate(outs):
            at = pl.ds(pl.multiple_of((place_ref[2] ^ m) * block, block), block)
            if stacked:
                out[:rows] = own_ref[:, at]
                out[rows:] = other_ref[:, at]
            else:
                out[...] = own_ref[:, at] + other_ref[:, at]

    return pl.pallas_call(
        kernel,
        in_specs=[scalar(), whole(), whole()],
        out_specs=[whole()] * devices,
        out_shape=[jax.ShapeDtypeStruct((tall, block), F32)] * devices,
        compiler_params=params(16),
        cost_estimate=BRIEF,
        name="spread",
    )(place, own, other)


def assemble(place, columns, base, blocks):
    rows = columns.shape[0]
    devices = len(blocks[0][2])
    width = blocks[0][2][0].shape[1]

    counts = [arrays[0].shape[0] for _, _, arrays in blocks]
    starts = starts_of(counts)

    given = [] if base is None else [base]

    def kernel(place_ref, columns_ref, *refs):
        out, value_ref, chosen_ref = refs[-3:]
        refs = refs[:-3]

        def chooser(kind, offset, count):
            wanted = lax.broadcasted_iota(jnp.int32, (rows, count), 1).astype(F32) + float(offset)
            return jnp.where(columns_ref[:, kind : kind + 1] == wanted, 1.0, 0.0).astype(BF16)

        for b, (start, count) in enumerate(zip(starts, counts)):
            for m in range(devices):
                value_ref[m, start : start + count] = refs[b * devices + m][...]
            chosen_ref[:, start : start + count] = chooser(blocks[b][0], blocks[b][1], count)

        def column(t, _):
            m, half = t // 2, pl.multiple_of(t % 2 * (rows // 2), rows // 2)
            at = pl.ds(pl.multiple_of((place_ref[2] ^ m) * width, width), width)
            total = pick(chosen_ref[pl.ds(half, rows // 2)], value_ref[m])
            out[pl.ds(half, rows // 2), at] = total + refs[-1][pl.ds(half, rows // 2), at] if given else total
            return 0

        lax.fori_loop(0, 2 * devices, column, 0)

    return pl.pallas_call(
        kernel,
        in_specs=[scalar(), whole()] + [whole()] * (devices * len(blocks) + len(given)),
        out_specs=whole(),
        out_shape=jax.ShapeDtypeStruct((rows, width * devices), F32),
        scratch_shapes=[pltpu.VMEM((devices, sum(counts), width), F32), pltpu.VMEM((rows, sum(counts)), BF16)],
        compiler_params=params(16),
        cost_estimate=BRIEF,
        name="assemble",
    )(place, columns, *[a for _, _, arrays in blocks for a in arrays], *given)


def swap_y(value, turn=0):
    return lax.ppermute(value, "redist", [(r, r ^ 2) for r in (*range(turn, 4), *range(turn))])


def swap_core(value):
    return lax.ppermute(value, "redist", [(r, r ^ 1) for r in range(4)])


def swap_z(value, m, devices):
    return lax.ppermute(value, "contract", [(z, z ^ m) for z in range(devices)])


def most_of(count):
    groups = lax.axis_size("groups")
    most = count
    for g in range(groups):
        for c in range(2):
            if g or c:
                pairs = [(4 * a + r, 4 * ((a + g) % groups) + (r ^ c)) for a in range(groups) for r in range(4)]
                most = jnp.maximum(most, lax.ppermute(count, ("groups", "redist"), pairs))
    return most


def home(value, m, devices):
    pairs = [(r * devices + z, (r ^ 2) * devices + (z ^ m)) for r in range(4) for z in range(devices)]
    return lax.ppermute(value, ("redist", "contract"), pairs)


def sum_z(blocks, devices):
    total = blocks[0]
    for m in FAR_FIRST[:-1]:
        total = total + swap_z(blocks[m], m, devices)
    return total


def reduce_z(place, own, mate, devices):
    return sum_z(spread(place, own, swap_core(mate), devices), devices)


def gather_z(quarter, devices):
    return [quarter] + [swap_z(quarter, m, devices) for m in range(1, devices)]


def join(value, *others):
    return lax.optimization_barrier((value, *others))[0]


def crossing(total, spare, own, mate, integrals, place, ranks, columns, labels, cap):
    rows = [swap_y(a[:total]) for a in spare]
    reduced = sum_z(own_rows(place, *ranks, own, mate, integrals, cap), RING)
    quarter = jnp.concatenate([reduced[: 2 * cap], swap_core(reduced[2 * cap :])], 0)
    kept = gather_z(quarter, RING)

    ahead = [(quarter,), kept, ()]
    totals = None
    for i, (start, part) in enumerate(zip(starts_of(PARTS), rows)):
        part = join(part, *ahead[i], *(totals or ()))
        totals = crossed_rows(place, labels, cap, [part], [swap_core(part)], integrals, start, totals, i + 1 == len(rows))
    base = assemble(place, columns, None, [(1, 0, kept)])
    quarter = reduce_z(place, *totals, RING)
    last = {m: home(quarter, m, RING) for m in FAR_FIRST}
    return assemble(place, columns, base, [(0, 0, [last[m] for m in range(RING)])])


def paired(amplitudes, pair_irrep, integrals):
    rows = amplitudes.shape[0]
    cap = rows // 4
    position = lax.axis_index("redist")
    place = jnp.stack([position // 2, position % 2, lax.axis_index("contract")]).astype(jnp.int32)
    ranks, columns, message = ranks_of(pair_irrep, place, cap)
    labels_own = swap_y(message)
    labels = (labels_own, swap_core(labels_own))
    pieces = [(0, 0, rows, start, parts) for start, parts in zip(starts_of(PARTS), PARTS)]
    spare = pack(amplitudes, ranks, pieces, "pack_rows")
    most = most_of(jnp.maximum(message, labels_own)[1:2, 0:128])
    classes = [c for c in CLASSES if c < rows] + [rows]
    at = jnp.sum(jnp.asarray(classes, F32) < most[0, 0]).astype(jnp.int32)
    mate = swap_core(amplitudes)
    branches = [functools.partial(crossing, c, cap=cap) for c in classes]
    return lax.switch(at, branches, spare, amplitudes, mate, integrals, place, (ranks, swap_core(ranks)), columns, labels)


def general(amplitudes, pair_irrep, integrals):
    redist_count = lax.axis_size("redist")
    irreps_here = max(1, IRREPS // redist_count)
    copies = max(1, redist_count // IRREPS)
    pair_rows, contract_width = amplitudes.shape
    capacity = pair_rows // 4
    block_cols = integrals.shape[1] // irreps_here
    labels = pair_irrep[:, 0]
    onehot = (labels[:, None] == jnp.arange(IRREPS, dtype=jnp.int32)[None, :]).astype(jnp.int32)
    rank_in = jnp.sum(jnp.cumsum(onehot, axis=0) * onehot, axis=1) - 1
    slot_of = labels * capacity + rank_in
    source_rows = (
        jnp.full((IRREPS * capacity,), pair_rows, jnp.int32).at[slot_of].set(jnp.arange(pair_rows, dtype=jnp.int32))
    )
    source_rows = jnp.repeat(source_rows.reshape(IRREPS, 1, capacity), copies, axis=1).reshape(-1)
    gathered = jnp.take(amplitudes, source_rows, axis=0, mode="fill", fill_value=0.0)
    outgoing = gathered.reshape(redist_count, irreps_here, capacity, contract_width)
    local_cols = integrals.reshape(contract_width, irreps_here, block_cols)
    partial_value = jnp.einsum(
        "risk,kiw->risw",
        lax.all_to_all(outgoing, "redist", split_axis=0, concat_axis=0, tiled=True),
        local_cols,
        precision=lax.Precision.HIGHEST,
        preferred_element_type=F32,
    )
    summed = lax.psum(partial_value, "contract")
    returned = lax.all_to_all(summed, "redist", split_axis=0, concat_axis=0, tiled=True)
    by_irrep = returned.reshape(IRREPS, copies, capacity, block_cols)
    return by_irrep[labels, :, rank_in].reshape(pair_rows, copies * block_cols)


def shards(amplitudes, pair_irrep, integrals):
    rows, width = amplitudes.shape
    cols = integrals.shape[1] // 2
    fits = lax.axis_size("redist") == 4 and lax.axis_size("contract") == RING and rows % 64 == 0
    if fits and width % (128 * EIGHTHS) == 0 and cols % (256 * RING) == 0:
        return paired(amplitudes, pair_irrep, integrals)
    return general(amplitudes, pair_irrep, integrals)


def solution(mesh):
    return jax.shard_map(
        shards,
        mesh=mesh,
        in_specs=(
            P(("groups", "redist"), "contract"),
            P(("groups", "redist"), None),
            P("contract", "redist"),
        ),
        out_specs=P(("groups", "redist"), None),
        check_vma=False,
    )
```

```python
import functools

import jax
import jax.numpy as jnp
from jax import lax
from jax.experimental import pallas as pl
from jax.experimental.pallas import tpu as pltpu
from jax.sharding import PartitionSpec as P

IRREPS = 8
F32 = jnp.float32
BF16 = jnp.bfloat16

CLASSES = (152, 168, 184, 200)
EIGHTHS = 8
PARTS = (5, 2, 1)
RING = 4
FAR_FIRST = (2, 3, 1, 0)

BRIEF = pl.CostEstimate(flops=1, bytes_accessed=1, transcendentals=0)

dot = functools.partial(jnp.dot, preferred_element_type=F32)


def halves(value):
    high = value.astype(BF16)
    return high, (value - high.astype(F32)).astype(BF16)


def pick(chosen, value):
    high, low = halves(value)
    return dot(chosen, high) + dot(chosen, low)


def starts_of(parts):
    return [sum(parts[:i]) for i in range(len(parts))]


def params(mebibytes):
    return pltpu.CompilerParams(vmem_limit_bytes=mebibytes << 20)


def whole():
    return pl.BlockSpec(memory_space=pltpu.VMEM)


def scalar():
    return pl.BlockSpec(memory_space=pltpu.SMEM)


def ranks_of(labels, place, cap):
    rows = labels.shape[0]

    def kernel(place_ref, labels_ref, row_ref, col_ref, message_ref):
        base = (4 * place_ref[0]).astype(F32)
        core = place_ref[1].astype(F32)
        down = lax.broadcasted_iota(jnp.int32, (rows, rows), 0)
        across = lax.broadcasted_iota(jnp.int32, (rows, rows), 1)
        label_c = labels_ref[...].astype(F32)
        label_r = jnp.sum(jnp.where(down == across, label_c, 0.0), axis=0, keepdims=True)

        def facts(label):
            local = label - base
            stays = (local >= 0) & (local < 4)
            owner = jnp.where(local >= 2, 1.0, 0.0)
            order = jnp.where(owner == core, 0.0, 2.0) + (local - 2 * owner)
            return stays, order * cap

        stays_c, slot_c = facts(label_c)
        stays_r, slot_r = facts(label_r)
        cross_c = jnp.where(stays_c, 0.0, 1.0)
        cross_r = jnp.where(stays_r, 0.0, 1.0)
        alike = jnp.where(label_c == label_r, 1.0, 0.0)
        ahead = down < across
        rank_r = jnp.sum(jnp.where(ahead, cross_c, 0.0), axis=0, keepdims=True)
        rank_c = jnp.sum(jnp.where(across < down, cross_r, 0.0), axis=1, keepdims=True)
        inner_r = jnp.sum(jnp.where(ahead, alike, 0.0), axis=0, keepdims=True)
        inner_c = jnp.sum(jnp.where(across < down, alike, 0.0), axis=1, keepdims=True)
        rank_r = jnp.where(stays_r, -1.0, rank_r)
        rank_c = jnp.where(stays_c, -1.0, rank_c)
        slot_r = jnp.where(stays_r, slot_r + inner_r, -1.0)
        slot_c = jnp.where(stays_c, slot_c + inner_c, -1.0)
        sub = lax.broadcasted_iota(jnp.int32, (8, rows), 0)
        row_ref[...] = jnp.where(sub == 0, rank_r, slot_r)
        lane = lax.broadcasted_iota(jnp.int32, (rows, 128), 1)
        col_ref[...] = jnp.where(lane == 0, rank_c, slot_c)
        sent = jnp.sum(jnp.where(rank_c == across.astype(F32), label_c + 1.0, 0.0), axis=0, keepdims=True) - 1.0
        count = jnp.sum(cross_r, axis=1, keepdims=True)
        message_ref[...] = jnp.where(sub == 0, sent, count)

    return pl.pallas_call(
        kernel,
        in_specs=[scalar(), whole()],
        out_specs=[whole()] * 3,
        out_shape=[
            jax.ShapeDtypeStruct((8, rows), F32),
            jax.ShapeDtypeStruct((rows, 128), F32),
            jax.ShapeDtypeStruct((8, rows), F32),
        ],
        compiler_params=params(16),
        name="ranks",
    )(place, labels)


def pack(amplitudes, ranks, pieces, name):
    rows, width = amplitudes.shape
    step = width // EIGHTHS
    cuts = sorted({p[3] for p in pieces} | {p[3] + p[4] for p in pieces})

    def kernel(ranks_ref, from_ref, *refs):
        outs, (value_ref, sems) = refs[: len(pieces)], refs[len(pieces) :]

        def bring(k):
            at = pl.ds(pl.multiple_of(k * step, step), step)
            return pltpu.make_async_copy(from_ref.at[:, at], value_ref.at[:, at], sems.at[k])

        def begin(k, _):
            bring(k).start()
            return 0

        lax.fori_loop(0, EIGHTHS, begin, 0)
        for low_cut, high_cut in zip(cuts, cuts[1:]):
            active = [(p, out) for p, out in zip(pieces, outs) if p[3] <= low_cut < p[3] + p[4]]
            if not active:
                continue
            chosen = []
            for (kind, offset, count, _, _), _ in active:
                wanted = lax.broadcasted_iota(jnp.int32, (count, rows), 0).astype(F32) + float(offset)
                chosen.append(jnp.where(ranks_ref[kind : kind + 1, :] == wanted, 1.0, 0.0).astype(BF16))
            chosen = jnp.concatenate(chosen, 0)

            def column(k, _):
                bring(k).wait()
                high, low = halves(value_ref[:, pl.ds(pl.multiple_of(k * step, step), step)])
                found = dot(chosen, high) + dot(chosen, low)
                at = 0
                for (_, _, count, start, _), out in active:
                    out[0:count, pl.ds(pl.multiple_of((k - start) * step, step), step)] = found[at : at + count]
                    at += count
                return 0

            lax.fori_loop(low_cut, high_cut, column, 0)

    return pl.pallas_call(
        kernel,
        in_specs=[whole(), pl.BlockSpec(memory_space=pl.ANY)],
        out_specs=[whole()] * len(pieces),
        out_shape=[jax.ShapeDtypeStruct((p[2], p[4] * step), F32) for p in pieces],
        scratch_shapes=[pltpu.VMEM((rows, width), F32), pltpu.SemaphoreType.DMA((EIGHTHS,))],
        compiler_params=params(16),
        cost_estimate=BRIEF,
        name=name,
    )(ranks, amplitudes)


def own_rows(place, ranks_own, ranks_mate, own, mate, integrals, cap):
    rows, width = own.shape
    slots = 2 * cap
    cols = integrals.shape[1] // 2
    block = cols // RING
    step = width // EIGHTHS
    tile = min(512, cols)
    per = cols // tile

    def kernel(place_ref, ranks_own_ref, ranks_mate_ref, own_ref, mate_ref, right_ref, *refs):
        outs, sum_ref, left_ref = refs[:RING], refs[RING], refs[RING + 1]

        @pl.when(pl.program_id(0) == 0)
        def _():
            sum_ref[...] = jnp.zeros_like(sum_ref)

        for p, (ranks_ref, value_ref) in enumerate(((ranks_own_ref, own_ref), (ranks_mate_ref, mate_ref))):
            wanted = lax.broadcasted_iota(jnp.int32, (slots, rows), 0).astype(F32) + float(p * slots)
            chosen = jnp.where(ranks_ref[1:2, :] == wanted, 1.0, 0.0).astype(BF16)
            for h, part in enumerate(halves(value_ref[...])):
                found = dot(chosen, part).astype(BF16)
                to = (2 * h + p) * cap
                for j in range(2):
                    left_ref[j, to : to + cap] = found[j * cap : (j + 1) * cap]

        def column(t, _):
            j = t // per
            high, low = halves(right_ref[:, pl.ds(pl.multiple_of(t * tile, tile), tile)])
            both = dot(left_ref[j], high)
            both = both[:slots] + both[slots:] + dot(left_ref[j, :slots], low)
            to = pl.ds(pl.multiple_of((t % per) * tile, tile), tile)
            sum_ref[pl.ds(pl.multiple_of(j * cap, cap), cap), to] += both[:cap]
            sum_ref[pl.ds(pl.multiple_of(slots + j * cap, cap), cap), to] += both[cap:]
            return 0

        lax.fori_loop(0, 2 * per, column, 0)

        @pl.when(pl.program_id(0) == pl.num_programs(0) - 1)
        def _():
            for m, out in enumerate(outs):
                out[...] = sum_ref[:, pl.ds(pl.multiple_of((place_ref[2] ^ m) * block, block), block)]

    ranks_spec = pl.BlockSpec((8, rows), lambda k: (0, 0))
    rows_spec = pl.BlockSpec((rows, step), lambda k: (0, k))
    return pl.pallas_call(
        kernel,
        grid=(EIGHTHS,),
        in_specs=[scalar(), ranks_spec, ranks_spec, rows_spec, rows_spec, pl.BlockSpec((step, 2 * cols), lambda k: (k, 0))],
        out_specs=[pl.BlockSpec((2 * slots, block), lambda k: (0, 0))] * RING,
        out_shape=[jax.ShapeDtypeStruct((2 * slots, block), F32)] * RING,
        scratch_shapes=[pltpu.VMEM((2 * slots, cols), F32), pltpu.VMEM((2, 2 * slots, step), BF16)],
        compiler_params=params(32),
        cost_estimate=BRIEF,
        name="own_rows",
    )(place, ranks_own, ranks_mate, own, mate, integrals)


def crossed_rows(place, labels, cap, own, mate, integrals, start, totals, final):
    count, width = sum(a.shape[0] for a in own), own[0].shape[1]
    cols = integrals.shape[1] // 2
    step = integrals.shape[0] // EIGHTHS
    pieces = len(own)
    ranks = 4 * cap
    tile = min(512, cols)
    per = cols // tile
    slotted = count > cap
    tall = cap if slotted else count
    held = 2 * cap if slotted else count
    earlier = [] if totals is None else list(totals)
    sorted_out = slotted and final

    def kernel(place_ref, labels_own_ref, labels_mate_ref, *refs):
        values = [jnp.concatenate([r[...] for r in refs[p * pieces : (p + 1) * pieces]], 0) for p in range(2)]
        right_ref, *refs = refs[2 * pieces :]
        before = refs[: len(earlier)]
        outs = refs[len(earlier) : len(earlier) + 2]
        left_ref = refs[len(earlier) + 2]
        sums = refs[len(earlier) + 3 :] if sorted_out else outs

        @pl.when(pl.program_id(0) == 0)
        def _():
            for i in range(2):
                sums[i][...] = before[i][...] if before else jnp.zeros_like(sums[i])

        wanted = lax.broadcasted_iota(jnp.int32, (count, ranks), 0)
        at = lax.broadcasted_iota(jnp.int32, (count, ranks), 1)
        first_irrep = (4 * place_ref[0] + 2 * place_ref[1]).astype(F32)
        label_c = [jnp.sum(jnp.where(wanted == at, r[0:1, :], 0.0), axis=1, keepdims=True) for r in (labels_own_ref, labels_mate_ref)]
        if slotted:
            down = lax.broadcasted_iota(jnp.int32, (count, count), 0)
            across = lax.broadcasted_iota(jnp.int32, (count, count), 1)
            label_r = [jnp.sum(jnp.where(down == across, c, 0.0), axis=0, keepdims=True) for c in label_c]
            rank_r = [
                jnp.sum(jnp.where((down < across) & (c == r), 1.0, 0.0), axis=0, keepdims=True) for c, r in zip(label_c, label_r)
            ]
            slot = lax.broadcasted_iota(jnp.int32, (cap, count), 0).astype(F32)
            parts = [halves(v) for v in values]
            for j in range(2):
                irrep = first_irrep + float(j)
                chosen = [jnp.where((r == irrep) & (k == slot), 1.0, 0.0).astype(BF16) for r, k in zip(label_r, rank_r)]
                for h in range(2):
                    for p in range(2):
                        to = (2 * h + p) * cap
                        left_ref[j, to : to + cap] = dot(chosen[p], parts[p][h]).astype(BF16)
        else:
            label = jnp.concatenate(label_c, 0)
            value = jnp.concatenate(values, 0)
            for j in range(2):
                left_ref[j] = jnp.concatenate(halves(jnp.where(label == first_irrep + float(j), value, 0.0)), 0)

        def column(t, _):
            j = t // per
            high, low = halves(right_ref[:, pl.ds(pl.multiple_of(t * tile, tile), tile)])
            both = dot(left_ref[j], high)
            both = both[: 2 * tall] + both[2 * tall :] + dot(left_ref[j, : 2 * tall], low)
            to = pl.ds(pl.multiple_of((t % per) * tile, tile), tile)
            rows = pl.ds(pl.multiple_of(j * cap, cap), cap) if slotted else slice(None)
            sums[0][rows, to] += both[:tall]
            sums[1][rows, to] += both[tall:]
            return 0

        lax.fori_loop(0, 2 * per, column, 0)

        if sorted_out:

            @pl.when(pl.program_id(0) == pl.num_programs(0) - 1)
            def _():
                slot = lax.broadcasted_iota(jnp.int32, (count, cap), 1).astype(F32)
                for p in range(2):
                    rank_c = jnp.sum(
                        jnp.where((across < down) & (label_c[p] == label_r[p]), 1.0, 0.0), axis=1, keepdims=True
                    )
                    chosen = [
                        jnp.where((label_c[p] == first_irrep + float(j)) & (rank_c == slot), 1.0, 0.0).astype(BF16) for j in range(2)
                    ]
                    chosen = jnp.concatenate(chosen, 1)

                    def back(t, _):
                        to = pl.ds(pl.multiple_of(t * 256, 256), 256)
                        outs[p][:, to] = pick(chosen, sums[p][:, to])
                        return 0

                    lax.fori_loop(0, cols // 256, back, 0)

    label_spec = pl.BlockSpec((8, ranks), lambda k: (0, 0))
    held_spec = pl.BlockSpec((held, cols), lambda k: (0, 0))
    given = count if final else held
    out_spec = pl.BlockSpec((given, cols), lambda k: (0, 0))
    return pl.pallas_call(
        kernel,
        grid=(width // step,),
        in_specs=[scalar(), label_spec, label_spec]
        + [pl.BlockSpec((a.shape[0], step), lambda k: (0, k)) for a in own + mate]
        + [pl.BlockSpec((step, 2 * cols), lambda k: (k + start, 0))]
        + [held_spec] * len(earlier),
        out_specs=[out_spec] * 2,
        out_shape=[jax.ShapeDtypeStruct((given, cols), F32)] * 2,
        scratch_shapes=[pltpu.VMEM((2, 4 * tall, step), BF16)] + [pltpu.VMEM((held, cols), F32)] * (2 if sorted_out else 0),
        compiler_params=params(32),
        cost_estimate=BRIEF,
        name="crossed_rows",
    )(place, *labels, *own, *mate, integrals, *earlier)


def spread(place, own, other, devices, stacked=False):
    rows, cols = own.shape
    block = cols // devices
    tall = 2 * rows if stacked else rows

    def kernel(place_ref, own_ref, other_ref, *outs):
        for m, out in enumerate(outs):
            at = pl.ds(pl.multiple_of((place_ref[2] ^ m) * block, block), block)
            if stacked:
                out[:rows] = own_ref[:, at]
                out[rows:] = other_ref[:, at]
            else:
                out[...] = own_ref[:, at] + other_ref[:, at]

    return pl.pallas_call(
        kernel,
        in_specs=[scalar(), whole(), whole()],
        out_specs=[whole()] * devices,
        out_shape=[jax.ShapeDtypeStruct((tall, block), F32)] * devices,
        compiler_params=params(16),
        cost_estimate=BRIEF,
        name="spread",
    )(place, own, other)


def assemble(place, columns, base, blocks):
    rows = columns.shape[0]
    devices = len(blocks[0][2])
    width = blocks[0][2][0].shape[1]

    counts = [arrays[0].shape[0] for _, _, arrays in blocks]
    starts = starts_of(counts)

    given = [] if base is None else [base]

    def kernel(place_ref, columns_ref, *refs):
        out, value_ref, chosen_ref = refs[-3:]
        refs = refs[:-3]

        def chooser(kind, offset, count):
            wanted = lax.broadcasted_iota(jnp.int32, (rows, count), 1).astype(F32) + float(offset)
            return jnp.where(columns_ref[:, kind : kind + 1] == wanted, 1.0, 0.0).astype(BF16)

        for b, (start, count) in enumerate(zip(starts, counts)):
            for m in range(devices):
                value_ref[m, start : start + count] = refs[b * devices + m][...]
            chosen_ref[:, start : start + count] = chooser(blocks[b][0], blocks[b][1], count)

        def column(t, _):
            m, half = t // 2, pl.multiple_of(t % 2 * (rows // 2), rows // 2)
            at = pl.ds(pl.multiple_of((place_ref[2] ^ m) * width, width), width)
            total = pick(chosen_ref[pl.ds(half, rows // 2)], value_ref[m])
            out[pl.ds(half, rows // 2), at] = total + refs[-1][pl.ds(half, rows // 2), at] if given else total
            return 0

        lax.fori_loop(0, 2 * devices, column, 0)

    return pl.pallas_call(
        kernel,
        in_specs=[scalar(), whole()] + [whole()] * (devices * len(blocks) + len(given)),
        out_specs=whole(),
        out_shape=jax.ShapeDtypeStruct((rows, width * devices), F32),
        scratch_shapes=[pltpu.VMEM((devices, sum(counts), width), F32), pltpu.VMEM((rows, sum(counts)), BF16)],
        compiler_params=params(16),
        cost_estimate=BRIEF,
        name="assemble",
    )(place, columns, *[a for _, _, arrays in blocks for a in arrays], *given)


def swap_y(value, turn=0):
    return lax.ppermute(value, "redist", [(r, r ^ 2) for r in (*range(turn, 4), *range(turn))])


def swap_core(value):
    return lax.ppermute(value, "redist", [(r, r ^ 1) for r in range(4)])


def swap_z(value, m, devices):
    return lax.ppermute(value, "contract", [(z, z ^ m) for z in range(devices)])


def most_of(count):
    groups = lax.axis_size("groups")
    most = count
    for g in range(groups):
        for c in range(2):
            if g or c:
                pairs = [(4 * a + r, 4 * ((a + g) % groups) + (r ^ c)) for a in range(groups) for r in range(4)]
                most = jnp.maximum(most, lax.ppermute(count, ("groups", "redist"), pairs))
    return most


def home(value, m, devices):
    pairs = [(r * devices + z, (r ^ 2) * devices + (z ^ m)) for r in range(4) for z in range(devices)]
    return lax.ppermute(value, ("redist", "contract"), pairs)


def sum_z(blocks, devices):
    total = blocks[0]
    for m in FAR_FIRST[:-1]:
        total = total + swap_z(blocks[m], m, devices)
    return total


def reduce_z(place, own, mate, devices):
    return sum_z(spread(place, own, swap_core(mate), devices), devices)


def gather_z(quarter, devices):
    return [quarter] + [swap_z(quarter, m, devices) for m in range(1, devices)]


def join(value, *others):
    return lax.optimization_barrier((value, *others))[0]


def crossing(total, spare, own, mate, integrals, place, ranks, columns, labels, cap):
    rows = [swap_y(a[:total]) for a in spare]
    reduced = sum_z(own_rows(place, *ranks, own, mate, integrals, cap), RING)
    quarter = jnp.concatenate([reduced[: 2 * cap], swap_core(reduced[2 * cap :])], 0)
    kept = gather_z(quarter, RING)

    ahead = [(quarter,), kept, ()]
    totals = None
    for i, (start, part) in enumerate(zip(starts_of(PARTS), rows)):
        part = join(part, *ahead[i], *(totals or ()))
        totals = crossed_rows(place, labels, cap, [part], [swap_core(part)], integrals, start, totals, i + 1 == len(rows))
    base = assemble(place, columns, None, [(1, 0, kept)])
    quarter = reduce_z(place, *totals, RING)
    last = {m: home(quarter, m, RING) for m in FAR_FIRST}
    return assemble(place, columns, base, [(0, 0, [last[m] for m in range(RING)])])


def paired(amplitudes, pair_irrep, integrals):
    rows = amplitudes.shape[0]
    cap = rows // 4
    position = lax.axis_index("redist")
    place = jnp.stack([position // 2, position % 2, lax.axis_index("contract")]).astype(jnp.int32)
    ranks, columns, message = ranks_of(pair_irrep, place, cap)
    labels_own = swap_y(message)
    labels = (labels_own, swap_core(labels_own))
    pieces = [(0, 0, rows, start, parts) for start, parts in zip(starts_of(PARTS), PARTS)]
    spare = pack(amplitudes, ranks, pieces, "pack_rows")
    most = most_of(jnp.maximum(message, labels_own)[1:2, 0:128])
    classes = [c for c in CLASSES if c < rows] + [rows]
    at = jnp.sum(jnp.asarray(classes, F32) < most[0, 0]).astype(jnp.int32)
    mate = swap_core(amplitudes)
    branches = [functools.partial(crossing, c, cap=cap) for c in classes]
    return lax.switch(at, branches, spare, amplitudes, mate, integrals, place, (ranks, swap_core(ranks)), columns, labels)


def general(amplitudes, pair_irrep, integrals):
    redist_count = lax.axis_size("redist")
    irreps_here = max(1, IRREPS // redist_count)
    copies = max(1, redist_count // IRREPS)
    pair_rows, contract_width = amplitudes.shape
    capacity = pair_rows // 4
    block_cols = integrals.shape[1] // irreps_here
    labels = pair_irrep[:, 0]
    onehot = (labels[:, None] == jnp.arange(IRREPS, dtype=jnp.int32)[None, :]).astype(jnp.int32)
    rank_in = jnp.sum(jnp.cumsum(onehot, axis=0) * onehot, axis=1) - 1
    slot_of = labels * capacity + rank_in
    source_rows = (
        jnp.full((IRREPS * capacity,), pair_rows, jnp.int32).at[slot_of].set(jnp.arange(pair_rows, dtype=jnp.int32))
    )
    source_rows = jnp.repeat(source_rows.reshape(IRREPS, 1, capacity), copies, axis=1).reshape(-1)
    gathered = jnp.take(amplitudes, source_rows, axis=0, mode="fill", fill_value=0.0)
    outgoing = gathered.reshape(redist_count, irreps_here, capacity, contract_width)
    local_cols = integrals.reshape(contract_width, irreps_here, block_cols)
    partial_value = jnp.einsum(
        "risk,kiw->risw",
        lax.all_to_all(outgoing, "redist", split_axis=0, concat_axis=0, tiled=True),
        local_cols,
        precision=lax.Precision.HIGHEST,
        preferred_element_type=F32,
    )
    summed = lax.psum(partial_value, "contract")
    returned = lax.all_to_all(summed, "redist", split_axis=0, concat_axis=0, tiled=True)
    by_irrep = returned.reshape(IRREPS, copies, capacity, block_cols)
    return by_irrep[labels, :, rank_in].reshape(pair_rows, copies * block_cols)


def shards(amplitudes, pair_irrep, integrals):
    rows, width = amplitudes.shape
    cols = integrals.shape[1] // 2
    fits = lax.axis_size("redist") == 4 and lax.axis_size("contract") == RING and rows % 64 == 0
    if fits and width % (128 * EIGHTHS) == 0 and cols % (256 * RING) == 0:
        return paired(amplitudes, pair_irrep, integrals)
    return general(amplitudes, pair_irrep, integrals)


def solution(mesh):
    return jax.shard_map(
        shards,
        mesh=mesh,
        in_specs=(
            P(("groups", "redist"), "contract"),
            P(("groups", "redist"), None),
            P("contract", "redist"),
        ),
        out_specs=P(("groups", "redist"), None),
        check_vma=False,
    )
```

```python
import functools

import jax
import jax.numpy as jnp
from jax import lax
from jax.experimental import pallas as pl
from jax.experimental.pallas import tpu as pltpu
from jax.sharding import PartitionSpec as P

IRREPS = 8
F32 = jnp.float32
BF16 = jnp.bfloat16

CLASSES = (152, 160, 168, 184, 200)
EIGHTHS = 8
PARTS = (6, 2)
RING = 4
FAR_FIRST = (2, 3, 1, 0)

BRIEF = pl.CostEstimate(flops=1, bytes_accessed=1, transcendentals=0)

dot = functools.partial(jnp.dot, preferred_element_type=F32)


def halves(value):
    high = value.astype(BF16)
    return high, (value - high.astype(F32)).astype(BF16)


def pick(chosen, value):
    high, low = halves(value)
    return dot(chosen, high) + dot(chosen, low)


def starts_of(parts):
    return [sum(parts[:i]) for i in range(len(parts))]


def params(mebibytes):
    return pltpu.CompilerParams(vmem_limit_bytes=mebibytes << 20)


def whole():
    return pl.BlockSpec(memory_space=pltpu.VMEM)


def scalar():
    return pl.BlockSpec(memory_space=pltpu.SMEM)


def ranks_of(labels, place, cap):
    rows = labels.shape[0]

    def kernel(place_ref, labels_ref, row_ref, col_ref, message_ref):
        base = (4 * place_ref[0]).astype(F32)
        core = place_ref[1].astype(F32)
        down = lax.broadcasted_iota(jnp.int32, (rows, rows), 0)
        across = lax.broadcasted_iota(jnp.int32, (rows, rows), 1)
        label_c = labels_ref[...].astype(F32)
        label_r = jnp.sum(jnp.where(down == across, label_c, 0.0), axis=0, keepdims=True)

        def facts(label):
            local = label - base
            stays = (local >= 0) & (local < 4)
            owner = jnp.where(local >= 2, 1.0, 0.0)
            order = jnp.where(owner == core, 0.0, 2.0) + (local - 2 * owner)
            return stays, order * cap

        stays_c, slot_c = facts(label_c)
        stays_r, slot_r = facts(label_r)
        cross_c = jnp.where(stays_c, 0.0, 1.0)
        cross_r = jnp.where(stays_r, 0.0, 1.0)
        alike = jnp.where(label_c == label_r, 1.0, 0.0)
        ahead = down < across
        rank_r = jnp.sum(jnp.where(ahead, cross_c, 0.0), axis=0, keepdims=True)
        rank_c = jnp.sum(jnp.where(across < down, cross_r, 0.0), axis=1, keepdims=True)
        inner_r = jnp.sum(jnp.where(ahead, alike, 0.0), axis=0, keepdims=True)
        inner_c = jnp.sum(jnp.where(across < down, alike, 0.0), axis=1, keepdims=True)
        rank_r = jnp.where(stays_r, -1.0, rank_r)
        rank_c = jnp.where(stays_c, -1.0, rank_c)
        slot_r = jnp.where(stays_r, slot_r + inner_r, -1.0)
        slot_c = jnp.where(stays_c, slot_c + inner_c, -1.0)
        sub = lax.broadcasted_iota(jnp.int32, (8, rows), 0)
        row_ref[...] = jnp.where(sub == 0, rank_r, slot_r)
        lane = lax.broadcasted_iota(jnp.int32, (rows, 128), 1)
        col_ref[...] = jnp.where(lane == 0, rank_c, slot_c)
        sent = jnp.sum(jnp.where(rank_c == across.astype(F32), label_c + 1.0, 0.0), axis=0, keepdims=True) - 1.0
        count = jnp.sum(cross_r, axis=1, keepdims=True)
        message_ref[...] = jnp.where(sub == 0, sent, count)

    return pl.pallas_call(
        kernel,
        in_specs=[scalar(), whole()],
        out_specs=[whole()] * 3,
        out_shape=[
            jax.ShapeDtypeStruct((8, rows), F32),
            jax.ShapeDtypeStruct((rows, 128), F32),
            jax.ShapeDtypeStruct((8, rows), F32),
        ],
        compiler_params=params(16),
        name="ranks",
    )(place, labels)


def pack(amplitudes, ranks, pieces, name):
    rows, width = amplitudes.shape
    step = width // EIGHTHS
    cuts = sorted({p[3] for p in pieces} | {p[3] + p[4] for p in pieces})

    def kernel(ranks_ref, from_ref, *refs):
        outs, (value_ref, sems) = refs[: len(pieces)], refs[len(pieces) :]

        def bring(k):
            at = pl.ds(pl.multiple_of(k * step, step), step)
            return pltpu.make_async_copy(from_ref.at[:, at], value_ref.at[:, at], sems.at[k])

        def begin(k, _):
            bring(k).start()
            return 0

        lax.fori_loop(0, EIGHTHS, begin, 0)
        for low_cut, high_cut in zip(cuts, cuts[1:]):
            active = [(p, out) for p, out in zip(pieces, outs) if p[3] <= low_cut < p[3] + p[4]]
            if not active:
                continue
            chosen = []
            for (kind, offset, count, _, _), _ in active:
                wanted = lax.broadcasted_iota(jnp.int32, (count, rows), 0).astype(F32) + float(offset)
                chosen.append(jnp.where(ranks_ref[kind : kind + 1, :] == wanted, 1.0, 0.0).astype(BF16))
            chosen = jnp.concatenate(chosen, 0)

            def column(k, _):
                bring(k).wait()
                high, low = halves(value_ref[:, pl.ds(pl.multiple_of(k * step, step), step)])
                found = dot(chosen, high) + dot(chosen, low)
                at = 0
                for (_, _, count, start, _), out in active:
                    out[0:count, pl.ds(pl.multiple_of((k - start) * step, step), step)] = found[at : at + count]
                    at += count
                return 0

            lax.fori_loop(low_cut, high_cut, column, 0)

    return pl.pallas_call(
        kernel,
        in_specs=[whole(), pl.BlockSpec(memory_space=pl.ANY)],
        out_specs=[whole()] * len(pieces),
        out_shape=[jax.ShapeDtypeStruct((p[2], p[4] * step), F32) for p in pieces],
        scratch_shapes=[pltpu.VMEM((rows, width), F32), pltpu.SemaphoreType.DMA((EIGHTHS,))],
        compiler_params=params(16),
        cost_estimate=BRIEF,
        name=name,
    )(ranks, amplitudes)


def own_rows(place, ranks_own, ranks_mate, own, mate, integrals, cap):
    rows, width = own.shape
    slots = 2 * cap
    cols = integrals.shape[1] // 2
    block = cols // RING
    step = width // EIGHTHS
    tile = min(512, cols)
    per = cols // tile

    def kernel(place_ref, ranks_own_ref, ranks_mate_ref, own_ref, mate_ref, right_ref, *refs):
        outs, sum_ref, left_ref = refs[:RING], refs[RING], refs[RING + 1]

        @pl.when(pl.program_id(0) == 0)
        def _():
            sum_ref[...] = jnp.zeros_like(sum_ref)

        for p, (ranks_ref, value_ref) in enumerate(((ranks_own_ref, own_ref), (ranks_mate_ref, mate_ref))):
            wanted = lax.broadcasted_iota(jnp.int32, (slots, rows), 0).astype(F32) + float(p * slots)
            chosen = jnp.where(ranks_ref[1:2, :] == wanted, 1.0, 0.0).astype(BF16)
            for h, part in enumerate(halves(value_ref[...])):
                found = dot(chosen, part).astype(BF16)
                to = (2 * h + p) * cap
                for j in range(2):
                    left_ref[j, to : to + cap] = found[j * cap : (j + 1) * cap]

        def column(t, _):
            j = t // per
            high, low = halves(right_ref[:, pl.ds(pl.multiple_of(t * tile, tile), tile)])
            both = dot(left_ref[j], high)
            both = both[:slots] + both[slots:] + dot(left_ref[j, :slots], low)
            to = pl.ds(pl.multiple_of((t % per) * tile, tile), tile)
            sum_ref[pl.ds(pl.multiple_of(j * cap, cap), cap), to] += both[:cap]
            sum_ref[pl.ds(pl.multiple_of(slots + j * cap, cap), cap), to] += both[cap:]
            return 0

        lax.fori_loop(0, 2 * per, column, 0)

        @pl.when(pl.program_id(0) == pl.num_programs(0) - 1)
        def _():
            for m, out in enumerate(outs):
                out[...] = sum_ref[:, pl.ds(pl.multiple_of((place_ref[2] ^ m) * block, block), block)]

    ranks_spec = pl.BlockSpec((8, rows), lambda k: (0, 0))
    rows_spec = pl.BlockSpec((rows, step), lambda k: (0, k))
    return pl.pallas_call(
        kernel,
        grid=(EIGHTHS,),
        in_specs=[scalar(), ranks_spec, ranks_spec, rows_spec, rows_spec, pl.BlockSpec((step, 2 * cols), lambda k: (k, 0))],
        out_specs=[pl.BlockSpec((2 * slots, block), lambda k: (0, 0))] * RING,
        out_shape=[jax.ShapeDtypeStruct((2 * slots, block), F32)] * RING,
        scratch_shapes=[pltpu.VMEM((2 * slots, cols), F32), pltpu.VMEM((2, 2 * slots, step), BF16)],
        compiler_params=params(32),
        cost_estimate=BRIEF,
        name="own_rows",
    )(place, ranks_own, ranks_mate, own, mate, integrals)


def crossed_rows(place, labels, cap, own, mate, integrals, start, totals, final):
    count, width = sum(a.shape[0] for a in own), own[0].shape[1]
    cols = integrals.shape[1] // 2
    step = integrals.shape[0] // EIGHTHS
    pieces = len(own)
    ranks = 4 * cap
    tile = min(512, cols)
    per = cols // tile
    slotted = count > cap
    tall = cap if slotted else count
    held = 2 * cap if slotted else count
    earlier = [] if totals is None else list(totals)
    sorted_out = slotted and final

    def kernel(place_ref, labels_own_ref, labels_mate_ref, *refs):
        values = [jnp.concatenate([r[...] for r in refs[p * pieces : (p + 1) * pieces]], 0) for p in range(2)]
        right_ref, *refs = refs[2 * pieces :]
        before = refs[: len(earlier)]
        outs = refs[len(earlier) : len(earlier) + 2]
        left_ref = refs[len(earlier) + 2]
        sums = refs[len(earlier) + 3 :] if sorted_out else outs

        @pl.when(pl.program_id(0) == 0)
        def _():
            for i in range(2):
                sums[i][...] = before[i][...] if before else jnp.zeros_like(sums[i])

        wanted = lax.broadcasted_iota(jnp.int32, (count, ranks), 0)
        at = lax.broadcasted_iota(jnp.int32, (count, ranks), 1)
        first_irrep = (4 * place_ref[0] + 2 * place_ref[1]).astype(F32)
        label_c = [jnp.sum(jnp.where(wanted == at, r[0:1, :], 0.0), axis=1, keepdims=True) for r in (labels_own_ref, labels_mate_ref)]
        if slotted:
            down = lax.broadcasted_iota(jnp.int32, (count, count), 0)
            across = lax.broadcasted_iota(jnp.int32, (count, count), 1)
            label_r = [jnp.sum(jnp.where(down == across, c, 0.0), axis=0, keepdims=True) for c in label_c]
            rank_r = [
                jnp.sum(jnp.where((down < across) & (c == r), 1.0, 0.0), axis=0, keepdims=True) for c, r in zip(label_c, label_r)
            ]
            slot = lax.broadcasted_iota(jnp.int32, (cap, count), 0).astype(F32)
            parts = [halves(v) for v in values]
            for j in range(2):
                irrep = first_irrep + float(j)
                chosen = [jnp.where((r == irrep) & (k == slot), 1.0, 0.0).astype(BF16) for r, k in zip(label_r, rank_r)]
                for h in range(2):
                    for p in range(2):
                        to = (2 * h + p) * cap
                        left_ref[j, to : to + cap] = dot(chosen[p], parts[p][h]).astype(BF16)
        else:
            label = jnp.concatenate(label_c, 0)
            value = jnp.concatenate(values, 0)
            for j in range(2):
                left_ref[j] = jnp.concatenate(halves(jnp.where(label == first_irrep + float(j), value, 0.0)), 0)

        def column(t, _):
            j = t // per
            high, low = halves(right_ref[:, pl.ds(pl.multiple_of(t * tile, tile), tile)])
            both = dot(left_ref[j], high)
            both = both[: 2 * tall] + both[2 * tall :] + dot(left_ref[j, : 2 * tall], low)
            to = pl.ds(pl.multiple_of((t % per) * tile, tile), tile)
            rows = pl.ds(pl.multiple_of(j * cap, cap), cap) if slotted else slice(None)
            sums[0][rows, to] += both[:tall]
            sums[1][rows, to] += both[tall:]
            return 0

        lax.fori_loop(0, 2 * per, column, 0)

        if sorted_out:

            @pl.when(pl.program_id(0) == pl.num_programs(0) - 1)
            def _():
                slot = lax.broadcasted_iota(jnp.int32, (count, cap), 1).astype(F32)
                for p in range(2):
                    rank_c = jnp.sum(
                        jnp.where((across < down) & (label_c[p] == label_r[p]), 1.0, 0.0), axis=1, keepdims=True
                    )
                    chosen = [
                        jnp.where((label_c[p] == first_irrep + float(j)) & (rank_c == slot), 1.0, 0.0).astype(BF16) for j in range(2)
                    ]
                    chosen = jnp.concatenate(chosen, 1)

                    def back(t, _):
                        to = pl.ds(pl.multiple_of(t * 256, 256), 256)
                        outs[p][:, to] = pick(chosen, sums[p][:, to])
                        return 0

                    lax.fori_loop(0, cols // 256, back, 0)

    label_spec = pl.BlockSpec((8, ranks), lambda k: (0, 0))
    held_spec = pl.BlockSpec((held, cols), lambda k: (0, 0))
    given = count if final else held
    out_spec = pl.BlockSpec((given, cols), lambda k: (0, 0))
    return pl.pallas_call(
        kernel,
        grid=(width // step,),
        in_specs=[scalar(), label_spec, label_spec]
        + [pl.BlockSpec((a.shape[0], step), lambda k: (0, k)) for a in own + mate]
        + [pl.BlockSpec((step, 2 * cols), lambda k: (k + start, 0))]
        + [held_spec] * len(earlier),
        out_specs=[out_spec] * 2,
        out_shape=[jax.ShapeDtypeStruct((given, cols), F32)] * 2,
        scratch_shapes=[pltpu.VMEM((2, 4 * tall, step), BF16)] + [pltpu.VMEM((held, cols), F32)] * (2 if sorted_out else 0),
        compiler_params=params(32),
        cost_estimate=BRIEF,
        name="crossed_rows",
    )(place, *labels, *own, *mate, integrals, *earlier)


def spread(place, own, other, devices, stacked=False):
    rows, cols = own.shape
    block = cols // devices
    tall = 2 * rows if stacked else rows

    def kernel(place_ref, own_ref, other_ref, *outs):
        for m, out in enumerate(outs):
            at = pl.ds(pl.multiple_of((place_ref[2] ^ m) * block, block), block)
            if stacked:
                out[:rows] = own_ref[:, at]
                out[rows:] = other_ref[:, at]
            else:
                out[...] = own_ref[:, at] + other_ref[:, at]

    return pl.pallas_call(
        kernel,
        in_specs=[scalar(), whole(), whole()],
        out_specs=[whole()] * devices,
        out_shape=[jax.ShapeDtypeStruct((tall, block), F32)] * devices,
        compiler_params=params(16),
        cost_estimate=BRIEF,
        name="spread",
    )(place, own, other)


def assemble(place, columns, base, blocks):
    rows = columns.shape[0]
    devices = len(blocks[0][2])
    width = blocks[0][2][0].shape[1]

    counts = [arrays[0].shape[0] for _, _, arrays in blocks]
    starts = starts_of(counts)

    given = [] if base is None else [base]

    def kernel(place_ref, columns_ref, *refs):
        out, value_ref, chosen_ref = refs[-3:]
        refs = refs[:-3]

        def chooser(kind, offset, count):
            wanted = lax.broadcasted_iota(jnp.int32, (rows, count), 1).astype(F32) + float(offset)
            return jnp.where(columns_ref[:, kind : kind + 1] == wanted, 1.0, 0.0).astype(BF16)

        for b, (start, count) in enumerate(zip(starts, counts)):
            for m in range(devices):
                value_ref[m, start : start + count] = refs[b * devices + m][...]
            chosen_ref[:, start : start + count] = chooser(blocks[b][0], blocks[b][1], count)

        def column(t, _):
            m, half = t // 2, pl.multiple_of(t % 2 * (rows // 2), rows // 2)
            at = pl.ds(pl.multiple_of((place_ref[2] ^ m) * width, width), width)
            total = pick(chosen_ref[pl.ds(half, rows // 2)], value_ref[m])
            out[pl.ds(half, rows // 2), at] = total + refs[-1][pl.ds(half, rows // 2), at] if given else total
            return 0

        lax.fori_loop(0, 2 * devices, column, 0)

    return pl.pallas_call(
        kernel,
        in_specs=[scalar(), whole()] + [whole()] * (devices * len(blocks) + len(given)),
        out_specs=whole(),
        out_shape=jax.ShapeDtypeStruct((rows, width * devices), F32),
        scratch_shapes=[pltpu.VMEM((devices, sum(counts), width), F32), pltpu.VMEM((rows, sum(counts)), BF16)],
        compiler_params=params(16),
        cost_estimate=BRIEF,
        name="assemble",
    )(place, columns, *[a for _, _, arrays in blocks for a in arrays], *given)


def swap_y(value, turn=0):
    return lax.ppermute(value, "redist", [(r, r ^ 2) for r in (*range(turn, 4), *range(turn))])


def swap_core(value):
    return lax.ppermute(value, "redist", [(r, r ^ 1) for r in range(4)])


def swap_z(value, m, devices):
    return lax.ppermute(value, "contract", [(z, z ^ m) for z in range(devices)])


def most_of(count):
    groups = lax.axis_size("groups")
    most = count
    for g in range(groups):
        for c in range(2):
            if g or c:
                pairs = [(4 * a + r, 4 * ((a + g) % groups) + (r ^ c)) for a in range(groups) for r in range(4)]
                most = jnp.maximum(most, lax.ppermute(count, ("groups", "redist"), pairs))
    return most


def home(value, m, devices):
    pairs = [(r * devices + z, (r ^ 2) * devices + (z ^ m)) for r in range(4) for z in range(devices)]
    return lax.ppermute(value, ("redist", "contract"), pairs)


def sum_z(blocks, devices):
    total = blocks[0]
    for m in FAR_FIRST[:-1]:
        total = total + swap_z(blocks[m], m, devices)
    return total


def reduce_z(place, own, mate, devices):
    return sum_z(spread(place, own, swap_core(mate), devices), devices)


def gather_z(quarter, devices):
    return [quarter] + [swap_z(quarter, m, devices) for m in range(1, devices)]


def join(value, *others):
    return lax.optimization_barrier((value, *others))[0]


def crossing(total, spare, own, mate, integrals, place, ranks, columns, labels, cap):
    rows = [swap_y(a[:total]) for a in spare]
    reduced = sum_z(own_rows(place, *ranks, own, mate, integrals, cap), RING)
    quarter = jnp.concatenate([reduced[: 2 * cap], swap_core(reduced[2 * cap :])], 0)
    kept = gather_z(quarter, RING)

    ahead = [(quarter,), kept]
    totals = None
    for i, (start, part) in enumerate(zip(starts_of(PARTS), rows)):
        part = join(part, *ahead[i], *(totals or ()))
        totals = crossed_rows(place, labels, cap, [part], [swap_core(part)], integrals, start, totals, i + 1 == len(rows))
    base = assemble(place, columns, None, [(1, 0, kept)])
    quarter = reduce_z(place, *totals, RING)
    last = {m: home(quarter, m, RING) for m in FAR_FIRST}
    return assemble(place, columns, base, [(0, 0, [last[m] for m in range(RING)])])


def paired(amplitudes, pair_irrep, integrals):
    rows = amplitudes.shape[0]
    cap = rows // 4
    position = lax.axis_index("redist")
    place = jnp.stack([position // 2, position % 2, lax.axis_index("contract")]).astype(jnp.int32)
    ranks, columns, message = ranks_of(pair_irrep, place, cap)
    labels_own = swap_y(message)
    labels = (labels_own, swap_core(labels_own))
    pieces = [(0, 0, rows, start, parts) for start, parts in zip(starts_of(PARTS), PARTS)]
    spare = pack(amplitudes, ranks, pieces, "pack_rows")
    most = most_of(jnp.maximum(message, labels_own)[1:2, 0:128])
    classes = [c for c in CLASSES if c < rows] + [rows]
    at = jnp.sum(jnp.asarray(classes, F32) < most[0, 0]).astype(jnp.int32)
    mate = swap_core(amplitudes)
    branches = [functools.partial(crossing, c, cap=cap) for c in classes]
    return lax.switch(at, branches, spare, amplitudes, mate, integrals, place, (ranks, swap_core(ranks)), columns, labels)


def general(amplitudes, pair_irrep, integrals):
    redist_count = lax.axis_size("redist")
    irreps_here = max(1, IRREPS // redist_count)
    copies = max(1, redist_count // IRREPS)
    pair_rows, contract_width = amplitudes.shape
    capacity = pair_rows // 4
    block_cols = integrals.shape[1] // irreps_here
    labels = pair_irrep[:, 0]
    onehot = (labels[:, None] == jnp.arange(IRREPS, dtype=jnp.int32)[None, :]).astype(jnp.int32)
    rank_in = jnp.sum(jnp.cumsum(onehot, axis=0) * onehot, axis=1) - 1
    slot_of = labels * capacity + rank_in
    source_rows = (
        jnp.full((IRREPS * capacity,), pair_rows, jnp.int32).at[slot_of].set(jnp.arange(pair_rows, dtype=jnp.int32))
    )
    source_rows = jnp.repeat(source_rows.reshape(IRREPS, 1, capacity), copies, axis=1).reshape(-1)
    gathered = jnp.take(amplitudes, source_rows, axis=0, mode="fill", fill_value=0.0)
    outgoing = gathered.reshape(redist_count, irreps_here, capacity, contract_width)
    local_cols = integrals.reshape(contract_width, irreps_here, block_cols)
    partial_value = jnp.einsum(
        "risk,kiw->risw",
        lax.all_to_all(outgoing, "redist", split_axis=0, concat_axis=0, tiled=True),
        local_cols,
        precision=lax.Precision.HIGHEST,
        preferred_element_type=F32,
    )
    summed = lax.psum(partial_value, "contract")
    returned = lax.all_to_all(summed, "redist", split_axis=0, concat_axis=0, tiled=True)
    by_irrep = returned.reshape(IRREPS, copies, capacity, block_cols)
    return by_irrep[labels, :, rank_in].reshape(pair_rows, copies * block_cols)


def shards(amplitudes, pair_irrep, integrals):
    rows, width = amplitudes.shape
    cols = integrals.shape[1] // 2
    fits = lax.axis_size("redist") == 4 and lax.axis_size("contract") == RING and rows % 64 == 0
    if fits and width % (128 * EIGHTHS) == 0 and cols % (256 * RING) == 0:
        return paired(amplitudes, pair_irrep, integrals)
    return general(amplitudes, pair_irrep, integrals)


def solution(mesh):
    return jax.shard_map(
        shards,
        mesh=mesh,
        in_specs=(
            P(("groups", "redist"), "contract"),
            P(("groups", "redist"), None),
            P("contract", "redist"),
        ),
        out_specs=P(("groups", "redist"), None),
        check_vma=False,
    )
```
